128 devices in a mesh: gx: 16 (over z_lo, y, core), gy: 8 (over x, z_hi).
Axes of the slice: x: 4, y: 4, z: 4 (z_hi: 2, z_lo: 2; z = z_hi * 2 + z_lo), core: 2. Of those that a mesh axis runs over, the one named last changes fastest.
Arguments:
- queries: bfloat16 [64, 512, 1024], P('gy', 'gx'), may hold values from -8 to 8
- keys: bfloat16 [64, 512, 1024], P('gy', 'gx'), may hold values from -8 to 8
- values: bfloat16 [64, 512, 1024], P('gy', 'gx'), may hold values from -6 to 6
- out_grad: bfloat16 [64, 512, 1024], P('gy', 'gx'), may hold values from -6 to 6
- tissue: int32 [64, 512], P('gy', 'gx'), may hold values from 0 to 1, as said below
Outputs:
- attended: bfloat16 [64, 512, 1024], P('gy', 'gx')
- query_grad: bfloat16 [64, 512, 1024], P('gy', 'gx')
- key_grad: bfloat16 [64, 512, 1024], P('gy', 'gx')
- value_grad: bfloat16 [64, 512, 1024], P('gy', 'gx')
The draws below stay inside these ranges and needn't reach their ends.
Inputs may be any that keep to these rules, and one draw needn't show every extreme that they name: `tissue`: in each device's tile of 8 x 32 tokens the live tokens lie within one band of whole rows of the tile; the tile at the grid's first 8 rows and first 32 columns is all live.
All inputs are finite; a program needn't handle non-finite values.
Results may differ from the reference program's by a relative error of at most 0.039.
Values may be sent and summed in bfloat16 or wider, within the bound.
A program may use at most 128 MiB of HBM per device.

```python
import jax
import jax.numpy as jnp
from jax import lax

D = 1024
NH = 16
HD = 64
RAD = 6
TH = 8
TW = 32
H = 64
W = 512


def draw_queries(key, part):
    own_key = jax.random.fold_in(key, 3)
    return jnp.clip(jax.random.normal(own_key, (H, W, D), jnp.float32), -5.0, 5.0).astype(jnp.bfloat16)


def draw_keys(key, part):
    own_key = jax.random.fold_in(key, 4)
    return jnp.clip(jax.random.normal(own_key, (H, W, D), jnp.float32), -5.0, 5.0).astype(jnp.bfloat16)


def draw_tissue(key, part):
    key = jax.random.fold_in(key, 7)
    band_key, start_key, speckle_key = jax.random.split(key, 3)
    grid_rows = H // TH
    grid_cols = W // TW
    fewest_rows = max(1, TH // 16)
    band_height = jax.random.randint(band_key, (grid_rows, grid_cols), fewest_rows, TH + 1)
    start_raw = jax.random.randint(start_key, (grid_rows, grid_cols), 0, TH + 1)
    band_start = start_raw % (TH - band_height + 1)
    height_full = jnp.repeat(jnp.repeat(band_height, TH, axis=0), TW, axis=1)
    start_full = jnp.repeat(jnp.repeat(band_start, TH, axis=0), TW, axis=1)
    inner_row = (jnp.arange(H) % TH)[:, None]
    inside = (inner_row >= start_full) & (inner_row < start_full + height_full)
    speckle = jax.random.randint(speckle_key, (H, W), 0, 8) > 0
    corner = (jnp.arange(H)[:, None] < TH) & (jnp.arange(W)[None, :] < TW)
    return jnp.where(corner | inside & speckle, 1, 0).astype(jnp.int32)


def steps_of(stream_key, shape, cuts, least, high):
    def one(position, shards_of):
        heights = jax.random.uniform(jax.random.fold_in(jax.random.fold_in(stream_key, 6), position), (shards_of,), jnp.float32, least / len(cuts), high / len(cuts))
        return jnp.repeat(jnp.exp(heights), shape[position] // shards_of).reshape((-1,) + (1,) * (len(shape) - position - 1))

    level = one(*cuts[0])
    for cut in cuts[1:]:
        level = level * one(*cut)
    return level


def normal_values(key, dims, width, limit, shards=(), kind=jnp.bfloat16):
    factor_of = steps_of(key, dims, shards, -0.22, 0.18) if shards else 1.0
    result = jax.random.normal(key, dims, jnp.float32) * width * factor_of
    return jnp.minimum(jnp.maximum(result, -limit), limit).astype(kind)


def setup_inputs(seed: int = 0) -> dict:
    arg_keys = jax.random.split(jax.random.key(seed), 6)
    return {
        "queries": draw_queries(jax.random.fold_in(arg_keys[5], 71), 0),
        "keys": draw_keys(jax.random.fold_in(arg_keys[5], 71), 0),
        "values": normal_values(arg_keys[2], (H, W, D), 1.0, 6.0, ((0, 8), (1, 16))),
        "out_grad": normal_values(arg_keys[3], (H, W, D), 1.0, 6.0, ((0, 8), (1, 16))),
        "tissue": draw_tissue(jax.random.fold_in(arg_keys[5], 71), 0),
    }


def rounded_copy(array_in):
    return lax.optimization_barrier(array_in.astype(jnp.bfloat16)).astype(jnp.float32)


def reference(queries, keys, values, out_grad, tissue):
    head_count = NH
    head_size = HD
    model_width = D
    radius = RAD
    window_span = 2 * radius + 1
    band_rows = 8
    score_scale = head_size ** -0.5
    edges = ((radius, radius), (radius, radius), (0, 0))
    key_pad = jnp.pad(keys.astype(jnp.float32), edges)
    value_pad = jnp.pad(values.astype(jnp.float32), edges)
    live_map = (tissue > 0).astype(jnp.float32)
    live_pad = jnp.pad(live_map, edges[:2])
    query_all = queries.astype(jnp.float32)
    grad_all = out_grad.astype(jnp.float32)
    region_shape = (band_rows + 2 * radius, W + 2 * radius, model_width)
    steps_all = window_span * window_span

    def band_step(sums_so_far, band_index):
        key_sums, value_sums = sums_so_far
        anchor = jnp.zeros((), jnp.int32)
        top_row = (band_index * band_rows).astype(jnp.int32)
        band_shape = (band_rows, W, head_count, head_size)
        query_band = lax.dynamic_slice(query_all, (top_row, anchor, anchor), (band_rows, W, model_width)).reshape(band_shape)
        grad_band = lax.dynamic_slice(grad_all, (top_row, anchor, anchor), (band_rows, W, model_width)).reshape(band_shape)
        query_live = lax.dynamic_slice(live_map, (top_row, anchor), (band_rows, W)) > 0
        key_region = lax.dynamic_slice(key_pad, (top_row, anchor, anchor), region_shape)
        value_region = lax.dynamic_slice(value_pad, (top_row, anchor, anchor), region_shape)
        live_region = lax.dynamic_slice(live_pad, (top_row, anchor), region_shape[:2])

        def shifted(offset):
            row_shift = (offset // window_span).astype(jnp.int32)
            col_shift = (offset % window_span).astype(jnp.int32)
            key_part = lax.dynamic_slice(key_region, (row_shift, col_shift, anchor), (band_rows, W, model_width)).reshape(band_shape)
            value_part = lax.dynamic_slice(value_region, (row_shift, col_shift, anchor), (band_rows, W, model_width)).reshape(band_shape)
            allowed = lax.dynamic_slice(live_region, (row_shift, col_shift), (band_rows, W))[:, :, None] > 0
            scores = jnp.sum(query_band * key_part, axis=-1) * score_scale
            return scores, key_part, value_part, allowed, row_shift, col_shift

        def max_step(offset, running):
            scores, _, _, allowed, _, _ = shifted(offset)
            return jnp.maximum(running, jnp.where(allowed, scores, -1e30))

        top_score = lax.fori_loop(0, steps_all, max_step, jnp.full((band_rows, W, head_count), -1e30, jnp.float32))

        def sum_step(offset, running):
            scores, _, _, allowed, _, _ = shifted(offset)
            return running + jnp.where(allowed, jnp.exp(jnp.where(allowed, scores, -1e30) - top_score), 0.0)

        exp_total = lax.fori_loop(0, steps_all, sum_step, jnp.zeros((band_rows, W, head_count), jnp.float32))
        has_keys = exp_total > 0
        log_total = jnp.where(has_keys, top_score + jnp.log(jnp.where(has_keys, exp_total, 1.0)), 0.0)

        def attention_of(scores, allowed):
            keep = allowed & query_live[:, :, None]
            return jnp.where(keep, jnp.exp(jnp.where(keep, scores - log_total, -1e30)), 0.0)

        def out_step(offset, running):
            scores, _, value_part, allowed, _, _ = shifted(offset)
            weight = rounded_copy(attention_of(scores, allowed))
            return running + weight[..., None] * value_part

        out_sum = lax.fori_loop(0, steps_all, out_step, jnp.zeros(band_shape, jnp.float32))
        attended = out_sum.astype(jnp.bfloat16)
        row_delta = jnp.sum(attended.astype(jnp.float32) * grad_band, axis=-1)

        def back_step(offset, partial_sums):
            query_sum, key_band, value_band = partial_sums
            scores, key_part, value_part, allowed, row_shift, col_shift = shifted(offset)
            attention = attention_of(scores, allowed)
            weight = rounded_copy(attention)
            grad_prob = jnp.sum(grad_band * value_part, axis=-1)
            grad_score = rounded_copy(attention * (grad_prob - row_delta))
            query_sum = query_sum + grad_score[..., None] * key_part
            corner_at = (row_shift, col_shift, anchor)
            key_add = (grad_score[..., None] * query_band).reshape(band_rows, W, model_width)
            value_add = (weight[..., None] * grad_band).reshape(band_rows, W, model_width)
            key_band = lax.dynamic_update_slice(key_band, lax.dynamic_slice(key_band, corner_at, key_add.shape) + key_add, corner_at)
            value_band = lax.dynamic_update_slice(value_band, lax.dynamic_slice(value_band, corner_at, value_add.shape) + value_add, corner_at)
            return query_sum, key_band, value_band

        region_zero = jnp.zeros(region_shape, jnp.float32)
        query_sum, key_band, value_band = lax.fori_loop(0, steps_all, back_step, (jnp.zeros(band_shape, jnp.float32), region_zero, region_zero))
        place_at = (top_row, anchor, anchor)
        key_sums = lax.dynamic_update_slice(key_sums, lax.dynamic_slice(key_sums, place_at, region_shape) + key_band, place_at)
        value_sums = lax.dynamic_update_slice(value_sums, lax.dynamic_slice(value_sums, place_at, region_shape) + value_band, place_at)
        query_grad = (query_sum * score_scale).astype(jnp.bfloat16).reshape(band_rows, W, model_width)
        return (key_sums, value_sums), (attended.reshape(band_rows, W, model_width), query_grad)

    full_shape = (H + 2 * radius, W + 2 * radius, model_width)
    start_sums = (jnp.zeros(full_shape, jnp.float32), jnp.zeros(full_shape, jnp.float32))
    (key_sums, value_sums), (attended, query_grad) = lax.scan(band_step, start_sums, jnp.arange(H // band_rows, dtype=jnp.int32))
    attended = attended.reshape(H, W, model_width)
    query_grad = query_grad.reshape(H, W, model_width)
    key_grad = (key_sums[radius:H + radius, radius:W + radius] * score_scale).astype(jnp.bfloat16)
    value_grad = value_sums[radius:H + radius, radius:W + radius].astype(jnp.bfloat16)
    return attended, query_grad, key_grad, value_grad
```

```python
import functools

import jax
import jax.numpy as jnp
from jax import lax
from jax.experimental import pallas as pl
from jax.experimental.pallas import tpu as pltpu
from jax.sharding import PartitionSpec as P

MESH = pl.DeviceIdType.MESH
HD = 64
RAD = 6
TH = 8
TW = 32
LANES = 128
OWN = TH * TW
STRIP = RAD * TW
CENTER = OWN + 2 * STRIP
SPAN = TH + 2 * RAD
SLOTS = 128
KEYS = CENTER + 2 * SLOTS
FAR = -1e30
BF = jnp.bfloat16
F32 = jnp.float32


def iota(shape, dim):
    return lax.broadcasted_iota(jnp.int32, shape, dim)


def slot_row(slot):
    return jnp.floor((slot.astype(F32) + 0.5) * (1.0 / RAD)).astype(jnp.int32)


def select_rows(shape, slot_dim):
    slot_all, token = iota(shape, slot_dim), iota(shape, 1 - slot_dim)
    right = slot_all >= SLOTS
    slot = jnp.where(right, slot_all - SLOTS, slot_all)
    row = slot_row(slot)
    col = slot - row * RAD + jnp.where(right, TW - RAD, 0)
    hit = (slot < SPAN * RAD) & (token == row * TW + col)
    return jnp.where(hit, 1.0, 0.0).astype(BF)


def key_features(row, col, tile_col, padded, dead_tile):
    count = row.shape[0]
    lane = iota((count, LANES), 1)
    tile_row = jnp.where(
        row < RAD, 16 + TH - RAD + row, jnp.where(row < RAD + TH, row - RAD, 32 + row - RAD - TH)
    )
    pick = jnp.where(lane == tile_row, 1.0, 0.0).astype(BF)
    dead = jnp.dot(pick, dead_tile, preferred_element_type=F32)
    dead_part = jnp.where(lane == tile_col, dead, 0.0)
    row_part = jnp.where(jnp.abs(row - RAD - (lane - 32)) > RAD, 1.0, 0.0)
    col_part = jnp.where(jnp.abs(col - (lane - 40)) > RAD, 1.0, 0.0)
    pad_part = jnp.where((lane == 72) & padded, 1.0, 0.0)
    out = jnp.where(
        lane < 32, dead_part, jnp.where(lane < 40, row_part, jnp.where(lane < 72, col_part, pad_part))
    )
    return (out * FAR).astype(BF)


def kernel(
    groups, nx, ny,
    k_hbm, v_hbm, q_hbm, g_hbm, tissue_ref,
    o_hbm, dq_hbm, dk_hbm, dv_hbm,
    kv, q_buf, g_buf, feat, qfeat, sel, sel_t, dead, dead32, live_q,
    hsend, centre, own, hret_out, hret_in, vret_out, vret_in,
    o_buf, dq_buf, dk_buf, dv_buf,
    in_sem, out_sem, vf_send, vf_recv, hf_send, hf_recv, hr_send, hr_recv, vr_send, vr_recv,
    lv_send, lv_recv, lh_send, lh_recv,
):
    gx, gy = lax.axis_index("gx"), lax.axis_index("gy")
    has_up, has_down = gy > 0, gy < ny - 1
    has_left, has_right = gx > 0, gx < nx - 1
    up = (gx, jnp.maximum(gy - 1, 0))
    down = (gx, jnp.minimum(gy + 1, ny - 1))
    left = (jnp.maximum(gx - 1, 0), gy)
    right = (jnp.minimum(gx + 1, nx - 1), gy)
    sides = ((has_up, up), (has_down, down), (has_left, left), (has_right, right))

    def lanes_of(g):
        return pl.ds(pl.multiple_of(g * LANES, LANES), LANES)

    def remote(src, dst, send, recv, where):
        return pltpu.make_async_remote_copy(
            src_ref=src, dst_ref=dst, send_sem=send, recv_sem=recv,
            device_id=where, device_id_type=MESH,
        )

    def loads(g):
        at = lanes_of(g)
        mid = pl.ds(STRIP, OWN)
        return [
            pltpu.make_async_copy(k_hbm.at[:, at], kv.at[g, mid, pl.ds(0, LANES)], in_sem.at[g, 0]),
            pltpu.make_async_copy(v_hbm.at[:, at], kv.at[g, mid, pl.ds(LANES, LANES)], in_sem.at[g, 1]),
            pltpu.make_async_copy(q_hbm.at[:, at], q_buf.at[g], in_sem.at[g, 2]),
            pltpu.make_async_copy(g_hbm.at[:, at], g_buf.at[g], in_sem.at[g, 3]),
        ]

    def store(g, n):
        buf, hbm = ((o_buf, o_hbm), (dq_buf, dq_hbm), (dk_buf, dk_hbm), (dv_buf, dv_hbm))[n]
        return pltpu.make_async_copy(buf.at[g], hbm.at[:, lanes_of(g)], out_sem.at[g, n])

    def v_forward(g, way):
        at = lanes_of(g)
        from_rows = pl.ds(0, STRIP) if way == 0 else pl.ds(OWN - STRIP, STRIP)
        to_rows = pl.ds(STRIP + OWN, STRIP) if way == 0 else pl.ds(0, STRIP)
        return [
            remote(
                hbm.at[from_rows, at], kv.at[g, to_rows, pl.ds(n * LANES, LANES)],
                vf_send.at[g, way, n], vf_recv.at[g, way, n], up if way == 0 else down,
            )
            for n, hbm in enumerate((k_hbm, v_hbm))
        ]

    def h_forward(g, way):
        to_rows = pl.ds(CENTER + (1 - way) * SLOTS, SLOTS)
        return remote(
            hsend.at[g, pl.ds(way * SLOTS, SLOTS)], kv.at[g, to_rows],
            hf_send.at[g, way], hf_recv.at[g, way], left if way == 0 else right,
        )

    def h_return(g, way):
        return remote(
            hret_out.at[g, pl.ds(way * SLOTS, SLOTS)], hret_in.at[g, pl.ds((1 - way) * SLOTS, SLOTS)],
            hr_send.at[g, way], hr_recv.at[g, way], left if way == 0 else right,
        )

    def v_return(g, way):
        return remote(
            vret_out.at[g, way], vret_in.at[g, way],
            vr_send.at[g, way], vr_recv.at[g, way], up if way == 0 else down,
        )

    def live_v(way):
        to_rows = pl.ds(32, 16) if way == 0 else pl.ds(16, 16)
        return remote(
            dead.at[0, pl.ds(0, 16)], dead.at[0, to_rows],
            lv_send.at[way], lv_recv.at[way], up if way == 0 else down,
        )

    def live_h(way):
        return remote(
            dead.at[0, pl.ds(0, 48)], dead.at[2 - way, pl.ds(0, 48)],
            lh_send.at[way], lh_recv.at[way], left if way == 0 else right,
        )

    v_to = (has_up, has_down)
    v_from = (has_down, has_up)
    h_to = (has_left, has_right)
    h_from = (has_right, has_left)

    def start_loads(g, carry):
        for copy in loads(g):
            copy.start()
        return carry

    lax.fori_loop(0, groups, start_loads, 0)

    dead32[...] = jnp.ones_like(dead32)
    dead32[pl.ds(0, TH), pl.ds(0, TW)] = jnp.where(tissue_ref[...] > 0, 0.0, 1.0)
    dead[...] = jnp.zeros_like(dead)
    dead[0, pl.ds(0, 16), :] = dead32[...].astype(BF)
    for here, tile, first, count in (
        (has_up, 0, 16, 16), (has_down, 0, 32, 16), (has_left, 1, 0, 48), (has_right, 2, 0, 48),
    ):
        @pl.when(jnp.logical_not(here))
        def _():
            dead[tile, pl.ds(first, count), :] = jnp.ones((count, LANES), BF)

    for here, first, count in (
        (has_up, 0, STRIP), (has_down, STRIP + OWN, STRIP),
        (has_left, CENTER, SLOTS), (has_right, CENTER + SLOTS, SLOTS),
    ):
        @pl.when(jnp.logical_not(here))
        def _():
            def clear(g, carry):
                kv[g, pl.ds(first, count), :] = jnp.zeros((count, 2 * LANES), BF)
                return carry

            lax.fori_loop(0, groups, clear, 0)

    for here, way in ((has_down, 0), (has_up, 1)):
        @pl.when(jnp.logical_not(here))
        def _():
            def clear(g, carry):
                vret_in[g, way] = jnp.zeros((STRIP, 2 * LANES), BF)
                return carry

            lax.fori_loop(0, groups, clear, 0)

    for here, first in ((has_left, 0), (has_right, SLOTS)):
        @pl.when(jnp.logical_not(here))
        def _():
            def clear(g, carry):
                hret_in[g, pl.ds(first, SLOTS), :] = jnp.zeros((SLOTS, 2 * LANES), BF)
                return carry

            lax.fori_loop(0, groups, clear, 0)

    barrier = pltpu.get_barrier_semaphore()
    for here, where in sides:
        @pl.when(here)
        def _():
            pl.semaphore_signal(barrier, inc=1, device_id=where, device_id_type=MESH)
    peers = sum(here.astype(jnp.int32) for here, _ in sides)
    pl.semaphore_wait(barrier, peers)

    for way in range(2):
        @pl.when(v_to[way])
        def _():
            live_v(way).start()

    def start_forward(g, carry):
        for way in range(2):
            @pl.when(v_to[way])
            def _():
                for copy in v_forward(g, way):
                    copy.start()
        return carry

    lax.fori_loop(0, groups, start_forward, 0)

    sel[...] = select_rows((2 * SLOTS, CENTER), 0)
    sel_t[...] = select_rows((CENTER, 2 * SLOTS), 1)
    token, lane = iota((OWN, LANES), 0), iota((OWN, LANES), 1)
    same = (
        (lane < 32)
        | ((lane >= 32) & (lane < 40) & (lane - 32 == token // TW))
        | ((lane >= 40) & (lane < 72) & (lane - 40 == token % TW))
        | (lane == 72)
    )
    qfeat[...] = jnp.where(same, 1.0, 0.0).astype(BF)

    for way in range(2):
        @pl.when(v_from[way])
        def _():
            live_v(way).wait_recv()
    for way in range(2):
        @pl.when(h_to[way])
        def _():
            live_h(way).start()

    tile = dead[0].astype(F32).T.astype(BF)
    row_of, token_of = iota((LANES, OWN), 0), iota((LANES, OWN), 1)
    pick = jnp.where(row_of == token_of // TW, 1.0, 0.0).astype(BF)
    spread = jnp.dot(tile, pick, preferred_element_type=F32)
    dead_q = jnp.sum(jnp.where(row_of == token_of % TW, spread, 0.0), axis=0, keepdims=True)
    live_q[...] = jnp.broadcast_to(1.0 - dead_q, (8, OWN))

    token = iota((CENTER, LANES), 0)
    feat[pl.ds(0, CENTER), :] = key_features(
        token // TW, token % TW, token % TW, token < 0, dead[0]
    )
    for way in range(2):
        @pl.when(h_from[way])
        def _():
            live_h(way).wait_recv()
    slot = iota((SLOTS, LANES), 0)
    row = slot_row(slot)
    col = slot - row * RAD
    none = slot >= SPAN * RAD
    feat[pl.ds(CENTER, SLOTS), :] = key_features(row, col - RAD, col + TW - RAD, none, dead[1])
    feat[pl.ds(CENTER + SLOTS, SLOTS), :] = key_features(row, col + TW, col, none, dead[2])

    def send_sides(g):
        for copy in loads(g):
            copy.wait()
        for way in range(2):
            @pl.when(v_from[way])
            def _():
                for copy in v_forward(g, way):
                    copy.wait_recv()
        picked = jnp.dot(sel[...], kv[g, pl.ds(0, CENTER), :], preferred_element_type=F32)
        hsend[g] = picked.astype(BF)
        for way in range(2):
            @pl.when(h_to[way])
            def _():
                h_forward(g, way).start()

    def attend(g):
        for way in range(2):
            @pl.when(h_from[way])
            def _():
                h_forward(g, way).wait_recv()
        key_all, value_all = kv[g, :, pl.ds(0, LANES)], kv[g, :, pl.ds(LANES, LANES)]
        key_t, value_t = key_all.T, value_all.T
        query = q_buf[g] * (HD ** -0.5)
        grad = g_buf[g]
        grad_t = grad.T.astype(F32)
        with_feat = jnp.concatenate([key_all, feat[...]], axis=1)
        head_of = iota((OWN, LANES), 1) // HD
        nothing = jnp.zeros((OWN, LANES), BF)
        live_row = live_q[pl.ds(0, 1), :]
        key_grad = value_grad = None
        attended_t, query_grad_t = [], []
        contract = (((1,), (1,)), ((), ()))
        for head in range(LANES // HD):
            part = slice(head * HD, (head + 1) * HD)
            query_h = jnp.where(head_of == head, query, nothing)
            grad_h = jnp.where(head_of == head, grad, nothing)
            scores = lax.dot_general(
                with_feat, jnp.concatenate([query_h, qfeat[...]], axis=1), contract,
                preferred_element_type=F32,
            )
            top = jnp.max(scores, axis=0, keepdims=True)
            raised = jnp.exp(scores - top)
            total = jnp.sum(raised, axis=0, keepdims=True)
            attention = raised * (live_row / total)
            weight = attention.astype(BF)
            out_t = jnp.dot(value_t[part], weight, preferred_element_type=F32).astype(BF).astype(F32)
            attended_t.append(out_t)
            row_delta = jnp.sum(out_t * grad_t[part], axis=0, keepdims=True)
            grad_prob = lax.dot_general(value_all, grad_h, contract, preferred_element_type=F32)
            grad_score = (attention * (grad_prob - row_delta)).astype(BF)
            query_grad_t.append(jnp.dot(key_t[part], grad_score, preferred_element_type=F32))
            key_add = jnp.dot(grad_score, query_h, preferred_element_type=F32)
            value_add = jnp.dot(weight, grad_h, preferred_element_type=F32)
            key_grad = key_add if key_grad is None else key_grad + key_add
            value_grad = value_add if value_grad is None else value_grad + value_add
        o_buf[g] = jnp.concatenate(attended_t, axis=0).T.astype(BF)
        dq_buf[g] = (jnp.concatenate(query_grad_t, axis=0) * (HD ** -0.5)).T.astype(BF)
        store(g, 0).start()
        store(g, 1).start()
        sums = jnp.concatenate([key_grad, value_grad], axis=1)
        centre[lax.rem(g, 2)] = sums[:CENTER]
        hret_out[g] = sums[CENTER:].astype(BF)
        for way in range(2):
            @pl.when(h_to[way])
            def _():
                h_return(g, way).start()

    def send_rows(g):
        for way in range(2):
            @pl.when(h_from[way])
            def _():
                h_return(g, way).wait_recv()
        sums = centre[lax.rem(g, 2)] + jnp.dot(sel_t[...], hret_in[g], preferred_element_type=F32)
        own[g] = sums[STRIP : STRIP + OWN]
        vret_out[g, 0] = sums[:STRIP].astype(BF)
        vret_out[g, 1] = sums[STRIP + OWN :].astype(BF)
        for way in range(2):
            @pl.when(v_to[way])
            def _():
                v_return(g, way).start()

    def step(i, carry):
        @pl.when(i < groups)
        def _():
            send_sides(i)

        @pl.when((i >= 1) & (i <= groups))
        def _():
            attend(i - 1)

        @pl.when(i >= 2)
        def _():
            send_rows(i - 2)

        return carry

    lax.fori_loop(0, groups + 2, step, 0)

    def finish(g, carry):
        for way in range(2):
            @pl.when(v_from[way])
            def _():
                v_return(g, way).wait_recv()
        own[g, pl.ds(OWN - STRIP, STRIP), :] += vret_in[g, 0].astype(F32)
        own[g, pl.ds(0, STRIP), :] += vret_in[g, 1].astype(F32)
        dk_buf[g] = own[g, :, pl.ds(0, LANES)].astype(BF)
        dv_buf[g] = own[g, :, pl.ds(LANES, LANES)].astype(BF)
        store(g, 2).start()
        store(g, 3).start()
        return carry

    lax.fori_loop(0, groups, finish, 0)

    def drain(g, carry):
        for n in range(4):
            store(g, n).wait()
        for way in range(2):
            @pl.when(v_to[way])
            def _():
                for copy in v_forward(g, way):
                    copy.wait_send()
                v_return(g, way).wait_send()

            @pl.when(h_to[way])
            def _():
                h_forward(g, way).wait_send()
                h_return(g, way).wait_send()
        return carry

    lax.fori_loop(0, groups, drain, 0)
    for way in range(2):
        @pl.when(v_to[way])
        def _():
            live_v(way).wait_send()

        @pl.when(h_to[way])
        def _():
            live_h(way).wait_send()


def per_device(queries, keys, values, out_grad, tissue):
    width = queries.shape[-1]
    groups = width // LANES
    flat = (OWN, width)
    any_spec = pl.BlockSpec(memory_space=pl.ANY)
    dma = pltpu.SemaphoreType.DMA
    outs = pl.pallas_call(
        functools.partial(kernel, groups, lax.axis_size("gx"), lax.axis_size("gy")),
        out_shape=[jax.ShapeDtypeStruct(flat, BF)] * 4,
        in_specs=[any_spec] * 4 + [pl.BlockSpec(memory_space=pltpu.VMEM)],
        out_specs=[any_spec] * 4,
        scratch_shapes=[
            pltpu.VMEM((groups, KEYS, 2 * LANES), BF),
            pltpu.VMEM((groups, OWN, LANES), BF),
            pltpu.VMEM((groups, OWN, LANES), BF),
            pltpu.VMEM((KEYS, LANES), BF),
            pltpu.VMEM((OWN, LANES), BF),
            pltpu.VMEM((2 * SLOTS, CENTER), BF),
            pltpu.VMEM((CENTER, 2 * SLOTS), BF),
            pltpu.VMEM((3, LANES, LANES), BF),
            pltpu.VMEM((16, LANES), F32),
            pltpu.VMEM((8, OWN), F32),
            pltpu.VMEM((groups, 2 * SLOTS, 2 * LANES), BF),
            pltpu.VMEM((2, CENTER, 2 * LANES), F32),
            pltpu.VMEM((groups, OWN, 2 * LANES), F32),
            pltpu.VMEM((groups, 2 * SLOTS, 2 * LANES), BF),
            pltpu.VMEM((groups, 2 * SLOTS, 2 * LANES), BF),
            pltpu.VMEM((groups, 2, STRIP, 2 * LANES), BF),
            pltpu.VMEM((groups, 2, STRIP, 2 * LANES), BF),
            pltpu.VMEM((groups, OWN, LANES), BF),
            pltpu.VMEM((groups, OWN, LANES), BF),
            pltpu.VMEM((groups, OWN, LANES), BF),
            pltpu.VMEM((groups, OWN, LANES), BF),
            dma((groups, 4)), dma((groups, 4)),
            dma((groups, 2, 2)), dma((groups, 2, 2)),
            dma((groups, 2)), dma((groups, 2)),
            dma((groups, 2)), dma((groups, 2)),
            dma((groups, 2)), dma((groups, 2)),
            dma((2,)), dma((2,)), dma((2,)), dma((2,)),
        ],
        compiler_params=pltpu.CompilerParams(
            collective_id=0, has_side_effects=True, vmem_limit_bytes=56 * 1024 * 1024
        ),
    )(
        keys.reshape(flat), values.reshape(flat), queries.reshape(flat), out_grad.reshape(flat),
        tissue,
    )
    return tuple(out.reshape(queries.shape) for out in outs)


def solution(mesh):
    tokens = P("gy", "gx", None)
    return jax.shard_map(
        per_device, mesh=mesh, in_specs=(tokens,) * 4 + (P("gy", "gx"),),
        out_specs=(tokens,) * 4, check_vma=False,
    )
```

```python
import functools

import jax
import jax.numpy as jnp
from jax import lax
from jax.experimental import pallas as pl
from jax.experimental.pallas import tpu as pltpu
from jax.sharding import PartitionSpec as P

MESH = pl.DeviceIdType.MESH
HD = 64
RAD = 6
TH = 8
TW = 32
LANES = 128
OWN = TH * TW
STRIP = RAD * TW
CENTER = OWN + 2 * STRIP
SPAN = TH + 2 * RAD
SLOTS = 128
KEYS = CENTER + 2 * SLOTS
FAR = -1e30
LEAD = 3
RATE = 1
BF = jnp.bfloat16
F32 = jnp.float32


def iota(shape, dim):
    return lax.broadcasted_iota(jnp.int32, shape, dim)


def slot_row(slot):
    return jnp.floor((slot.astype(F32) + 0.5) * (1.0 / RAD)).astype(jnp.int32)


def select_rows(shape, slot_dim):
    slot_all, token = iota(shape, slot_dim), iota(shape, 1 - slot_dim)
    right = slot_all >= SLOTS
    slot = jnp.where(right, slot_all - SLOTS, slot_all)
    row = slot_row(slot)
    col = slot - row * RAD + jnp.where(right, TW - RAD, 0)
    hit = (slot < SPAN * RAD) & (token == row * TW + col)
    return jnp.where(hit, 1.0, 0.0).astype(BF)


def key_features(row, col, tile_col, padded, dead_tile):
    count = row.shape[0]
    lane = iota((count, LANES), 1)
    tile_row = jnp.where(
        row < RAD, 16 + TH - RAD + row, jnp.where(row < RAD + TH, row - RAD, 32 + row - RAD - TH)
    )
    pick = jnp.where(lane == tile_row, 1.0, 0.0).astype(BF)
    dead = jnp.dot(pick, dead_tile, preferred_element_type=F32)
    dead_part = jnp.where(lane == tile_col, dead, 0.0)
    row_part = jnp.where(jnp.abs(row - RAD - (lane - 32)) > RAD, 1.0, 0.0)
    col_part = jnp.where(jnp.abs(col - (lane - 40)) > RAD, 1.0, 0.0)
    pad_part = jnp.where((lane == 72) & padded, 1.0, 0.0)
    out = jnp.where(
        lane < 32, dead_part, jnp.where(lane < 40, row_part, jnp.where(lane < 72, col_part, pad_part))
    )
    return (out * FAR).astype(BF)


def kernel(
    groups, nx, ny,
    k_hbm, v_hbm, q_hbm, g_hbm, tissue_ref,
    o_hbm, dq_hbm, dk_hbm, dv_hbm,
    kv, q_buf, g_buf, feat, qfeat, sel, sel_t, dead, dead32, live_q,
    hsend, centre, own, hret_out, hret_in, vret_out, vret_in,
    o_buf, dq_buf, dk_buf, dv_buf,
    row_relay, row_relay_back, side_relay, side_relay_back,
    in_sem, out_sem, vf_send, vf_recv, hf_send, hf_recv, hr_send, hr_recv, vr_send, vr_recv,
    lv_send, lv_recv, lh_send, lh_recv,
    rf_send, rf_recv, rb_send, rb_recv, sf_send, sf_recv, sb_send, sb_recv,
):
    gx, gy = lax.axis_index("gx"), lax.axis_index("gy")
    has_up, has_down = gy > 0, gy < ny - 1
    has_left, has_right = gx > 0, gx < nx - 1
    up = (gx, jnp.maximum(gy - 1, 0))
    down = (gx, jnp.minimum(gy + 1, ny - 1))
    left = (jnp.maximum(gx - 1, 0), gy)
    right = (jnp.minimum(gx + 1, nx - 1), gy)
    two_up = (gx, jnp.maximum(gy - 2, 0))
    two_down = (gx, jnp.minimum(gy + 2, ny - 1))

    def picked(g, count):
        inner = (g >= 1) & (g <= 6)
        even = lax.rem(g, 2) == 0
        half = ((g < 4) & jnp.logical_not(even)) | ((g >= 4) & even)
        return (
            ((count == 6) & inner) | ((count == 4) & inner & half) | ((count == 2) & ((g == 2) | (g == 5)))
        )

    even_row = lax.rem(gy, 2) == 0
    relayed_count = (jnp.where(even_row, gy, 0), jnp.where(even_row, 0, ny - 1 - gy))
    relay_for = (down, up)
    hand_count = jnp.where(even_row, ny - 2 - gy, gy - 1)

    def by_relay(g, way):
        return picked(g, relayed_count[way])

    def hands_on(g):
        return picked(g, hand_count)

    half = nx // 2
    seam = (gx == half - 1) | (gx == half)
    at_seam = ((gx == half), (gx == half - 1))
    routes = 3
    by_way = (tuple(2 * n for n in range(routes)), tuple(nx - 1 - 2 * n for n in range(routes)))

    def side_route(g):
        return jnp.where((g >= 1) & (g <= 6), 1 + lax.rem(g - 1, routes), 0)

    def relay_of(g, way):
        number = jnp.maximum(side_route(g) - 1, 0)
        return (2 * number if way == 0 else nx - 1 - 2 * number, gy)

    def side_picked(g):
        return side_route(g) > 0

    def hands_sides(g, way):
        return side_picked(g) & (gx == relay_of(g, way)[0])

    seam_to = ((half - 1, gy), (half, gy))
    on_route = (gx == by_way[0][0])
    for spot in by_way[0][1:] + by_way[1]:
        on_route = on_route | (gx == spot)

    sides = [
        (has_up, up), (has_down, down), (has_left, left), (has_right, right),
        (gy >= 2, two_up), (gy < ny - 2, two_down),
    ]
    sides += [(seam, (spot, gy)) for spot in by_way[0] + by_way[1]]
    sides += [(on_route, spot) for spot in seam_to]

    def lanes_of(g):
        return pl.ds(pl.multiple_of(g * LANES, LANES), LANES)

    def remote(src, dst, send, recv, where):
        return pltpu.make_async_remote_copy(
            src_ref=src, dst_ref=dst, send_sem=send, recv_sem=recv,
            device_id=where, device_id_type=MESH,
        )

    def loads(g):
        at = lanes_of(g)
        mid = pl.ds(STRIP, OWN)
        return [
            pltpu.make_async_copy(k_hbm.at[:, at], kv.at[g, mid, pl.ds(0, LANES)], in_sem.at[g, 0]),
            pltpu.make_async_copy(v_hbm.at[:, at], kv.at[g, mid, pl.ds(LANES, LANES)], in_sem.at[g, 1]),
            pltpu.make_async_copy(q_hbm.at[:, at], q_buf.at[g], in_sem.at[g, 2]),
            pltpu.make_async_copy(g_hbm.at[:, at], g_buf.at[g], in_sem.at[g, 3]),
        ]

    def store(g, n):
        buf, hbm = ((o_buf, o_hbm), (dq_buf, dq_hbm), (dk_buf, dk_hbm), (dv_buf, dv_hbm))[n]
        return pltpu.make_async_copy(buf.at[g], hbm.at[:, lanes_of(g)], out_sem.at[g, n])

    def v_forward(g, way):
        at = lanes_of(g)
        from_rows = pl.ds(0, STRIP) if way == 0 else pl.ds(OWN - STRIP, STRIP)
        to_rows = pl.ds(STRIP + OWN, STRIP) if way == 0 else pl.ds(0, STRIP)
        return [
            remote(
                hbm.at[from_rows, at], kv.at[g, to_rows, pl.ds(n * LANES, LANES)],
                vf_send.at[g, way, n], vf_recv.at[g, way, n], up if way == 0 else down,
            )
            for n, hbm in enumerate((k_hbm, v_hbm))
        ]

    def v_forward_first(g, way):
        at = lanes_of(g)
        from_rows = pl.ds(0, STRIP) if way == 0 else pl.ds(OWN - STRIP, STRIP)
        return [
            remote(
                hbm.at[from_rows, at], row_relay.at[g, :, pl.ds(n * LANES, LANES)],
                vf_send.at[g, way, n], rf_recv.at[g, n], relay_for[way],
            )
            for n, hbm in enumerate((k_hbm, v_hbm))
        ]

    def v_forward_second(g, way):
        to_rows = pl.ds(STRIP + OWN, STRIP) if way == 0 else pl.ds(0, STRIP)
        return [
            remote(
                row_relay.at[g, :, pl.ds(n * LANES, LANES)], kv.at[g, to_rows, pl.ds(n * LANES, LANES)],
                rf_send.at[g, n], vf_recv.at[g, way, n], two_up if way == 0 else two_down,
            )
            for n in range(2)
        ]

    def v_return_first(g, way):
        return remote(
            vret_out.at[g, way], row_relay_back.at[g],
            vr_send.at[g, way], rb_recv.at[g], relay_for[way],
        )

    def v_return_second(g, way):
        return remote(
            row_relay_back.at[g], vret_in.at[g, way],
            rb_send.at[g], vr_recv.at[g, way], two_up if way == 0 else two_down,
        )

    def h_forward_first(g, way):
        return remote(
            hsend.at[g, pl.ds(way * SLOTS, SLOTS)], side_relay.at[g],
            hf_send.at[g, way], sf_recv.at[g], relay_of(g, way),
        )

    def h_forward_second(g, way):
        to_rows = pl.ds(CENTER + (1 - way) * SLOTS, SLOTS)
        return remote(
            side_relay.at[g], kv.at[g, to_rows], sf_send.at[g], hf_recv.at[g, way], seam_to[way],
        )

    def h_return_first(g, way):
        return remote(
            hret_out.at[g, pl.ds(way * SLOTS, SLOTS)], side_relay_back.at[g],
            hr_send.at[g, way], sb_recv.at[g], relay_of(g, way),
        )

    def h_return_second(g, way):
        return remote(
            side_relay_back.at[g], hret_in.at[g, pl.ds((1 - way) * SLOTS, SLOTS)],
            sb_send.at[g], hr_recv.at[g, way], seam_to[way],
        )

    def h_forward(g, way):
        to_rows = pl.ds(CENTER + (1 - way) * SLOTS, SLOTS)
        return remote(
            hsend.at[g, pl.ds(way * SLOTS, SLOTS)], kv.at[g, to_rows],
            hf_send.at[g, way], hf_recv.at[g, way], left if way == 0 else right,
        )

    def h_return(g, way):
        return remote(
            hret_out.at[g, pl.ds(way * SLOTS, SLOTS)], hret_in.at[g, pl.ds((1 - way) * SLOTS, SLOTS)],
            hr_send.at[g, way], hr_recv.at[g, way], left if way == 0 else right,
        )

    def v_return(g, way):
        return remote(
            vret_out.at[g, way], vret_in.at[g, way],
            vr_send.at[g, way], vr_recv.at[g, way], up if way == 0 else down,
        )

    def live_v(way):
        to_rows = pl.ds(32, 16) if way == 0 else pl.ds(16, 16)
        return remote(
            dead.at[0, pl.ds(0, 16)], dead.at[0, to_rows],
            lv_send.at[way], lv_recv.at[way], up if way == 0 else down,
        )

    def live_h(way):
        return remote(
            dead.at[0, pl.ds(0, 48)], dead.at[2 - way, pl.ds(0, 48)],
            lh_send.at[way], lh_recv.at[way], left if way == 0 else right,
        )

    v_to = (has_up, has_down)
    v_from = (has_down, has_up)
    h_to = (has_left, has_right)
    h_from = (has_right, has_left)

    def send(here, special, direct, first):
        @pl.when(here & jnp.logical_not(special))
        def _():
            for copy in direct():
                copy.start()

        @pl.when(here & special)
        def _():
            for copy in first():
                copy.start()

    def start_rows(g):
        for way in range(2):
            send(
                v_to[way], by_relay(g, way),
                lambda: v_forward(g, way), lambda: v_forward_first(g, way),
            )

    def start_loads(g, carry):
        for copy in loads(g):
            copy.start()
        return carry

    lax.fori_loop(0, groups, start_loads, 0)

    dead32[...] = jnp.ones_like(dead32)
    dead32[pl.ds(0, TH), pl.ds(0, TW)] = jnp.where(tissue_ref[...] > 0, 0.0, 1.0)
    dead[...] = jnp.zeros_like(dead)
    dead[0, pl.ds(0, 16), :] = dead32[...].astype(BF)
    for here, tile, first, count in (
        (has_up, 0, 16, 16), (has_down, 0, 32, 16), (has_left, 1, 0, 48), (has_right, 2, 0, 48),
    ):
        @pl.when(jnp.logical_not(here))
        def _():
            dead[tile, pl.ds(first, count), :] = jnp.ones((count, LANES), BF)

    for here, first, count in (
        (has_up, 0, STRIP), (has_down, STRIP + OWN, STRIP),
        (has_left, CENTER, SLOTS), (has_right, CENTER + SLOTS, SLOTS),
    ):
        @pl.when(jnp.logical_not(here))
        def _():
            def clear(g, carry):
                kv[g, pl.ds(first, count), :] = jnp.zeros((count, 2 * LANES), BF)
                return carry

            lax.fori_loop(0, groups, clear, 0)

    for here, way in ((has_down, 0), (has_up, 1)):
        @pl.when(jnp.logical_not(here))
        def _():
            def clear(g, carry):
                vret_in[g, way] = jnp.zeros((STRIP, 2 * LANES), BF)
                return carry

            lax.fori_loop(0, groups, clear, 0)

    for here, first in ((has_left, 0), (has_right, SLOTS)):
        @pl.when(jnp.logical_not(here))
        def _():
            def clear(g, carry):
                hret_in[g, pl.ds(first, SLOTS), :] = jnp.zeros((SLOTS, 2 * LANES), BF)
                return carry

            lax.fori_loop(0, groups, clear, 0)

    barrier = pltpu.get_barrier_semaphore()
    for here, where in sides:
        @pl.when(here)
        def _():
            pl.semaphore_signal(barrier, inc=1, device_id=where, device_id_type=MESH)
    peers = sum(here.astype(jnp.int32) for here, _ in sides)
    pl.semaphore_wait(barrier, peers)

    for way in range(2):
        @pl.when(v_to[way])
        def _():
            live_v(way).start()

    def start_forward(g, carry):
        start_rows(g)
        return carry

    lax.fori_loop(0, LEAD, start_forward, 0)

    sel[...] = select_rows((2 * SLOTS, CENTER), 0)
    sel_t[...] = select_rows((CENTER, 2 * SLOTS), 1)
    token, lane = iota((OWN, LANES), 0), iota((OWN, LANES), 1)
    same = (
        (lane < 32)
        | ((lane >= 32) & (lane < 40) & (lane - 32 == token // TW))
        | ((lane >= 40) & (lane < 72) & (lane - 40 == token % TW))
        | (lane == 72)
    )
    qfeat[...] = jnp.where(same, 1.0, 0.0).astype(BF)

    for way in range(2):
        @pl.when(v_from[way])
        def _():
            live_v(way).wait_recv()
    for way in range(2):
        @pl.when(h_to[way])
        def _():
            live_h(way).start()

    tile = dead[0].astype(F32).T.astype(BF)
    row_of, token_of = iota((LANES, OWN), 0), iota((LANES, OWN), 1)
    pick = jnp.where(row_of == token_of // TW, 1.0, 0.0).astype(BF)
    spread = jnp.dot(tile, pick, preferred_element_type=F32)
    dead_q = jnp.sum(jnp.where(row_of == token_of % TW, spread, 0.0), axis=0, keepdims=True)
    live_q[...] = jnp.broadcast_to(1.0 - dead_q, (8, OWN))

    token = iota((CENTER, LANES), 0)
    feat[pl.ds(0, CENTER), :] = key_features(
        token // TW, token % TW, token % TW, token < 0, dead[0]
    )
    for way in range(2):
        @pl.when(h_from[way])
        def _():
            live_h(way).wait_recv()
    slot = iota((SLOTS, LANES), 0)
    row = slot_row(slot)
    col = slot - row * RAD
    none = slot >= SPAN * RAD
    feat[pl.ds(CENTER, SLOTS), :] = key_features(row, col - RAD, col + TW - RAD, none, dead[1])
    feat[pl.ds(CENTER + SLOTS, SLOTS), :] = key_features(row, col + TW, col, none, dead[2])

    def send_sides(g):
        for copy in loads(g):
            copy.wait()
        for way in range(2):
            @pl.when(v_from[way])
            def _():
                for copy in v_forward(g, way):
                    copy.wait_recv()
        picked = jnp.dot(sel[...], kv[g, pl.ds(0, CENTER), :], preferred_element_type=F32)
        hsend[g] = picked.astype(BF)
        for way in range(2):
            send(
                h_to[way], at_seam[way] & side_picked(g),
                lambda: [h_forward(g, way)], lambda: [h_forward_first(g, way)],
            )

    def attend(g):
        for way in range(2):
            @pl.when(h_from[way])
            def _():
                h_forward(g, way).wait_recv()
        key_all, value_all = kv[g, :, pl.ds(0, LANES)], kv[g, :, pl.ds(LANES, LANES)]
        key_t, value_t = key_all.T, value_all.T
        query = q_buf[g] * (HD ** -0.5)
        grad = g_buf[g]
        grad_t = grad.T.astype(F32)
        with_feat = jnp.concatenate([key_all, feat[...]], axis=1)
        head_of = iota((OWN, LANES), 1) // HD
        nothing = jnp.zeros((OWN, LANES), BF)
        live_row = live_q[pl.ds(0, 1), :]
        key_grad = value_grad = None
        attended_t, query_grad_t = [], []
        contract = (((1,), (1,)), ((), ()))
        for head in range(LANES // HD):
            part = slice(head * HD, (head + 1) * HD)
            query_h = jnp.where(head_of == head, query, nothing)
            grad_h = jnp.where(head_of == head, grad, nothing)
            scores = lax.dot_general(
                with_feat, jnp.concatenate([query_h, qfeat[...]], axis=1), contract,
                preferred_element_type=F32,
            )
            top = jnp.max(scores, axis=0, keepdims=True)
            raised = jnp.exp(scores - top)
            total = jnp.sum(raised, axis=0, keepdims=True)
            attention = raised * (live_row / total)
            weight = attention.astype(BF)
            out_t = jnp.dot(value_t[part], weight, preferred_element_type=F32).astype(BF).astype(F32)
            attended_t.append(out_t)
            row_delta = jnp.sum(out_t * grad_t[part], axis=0, keepdims=True)
            grad_prob = lax.dot_general(value_all, grad_h, contract, preferred_element_type=F32)
            grad_score = (attention * (grad_prob - row_delta)).astype(BF)
            query_grad_t.append(jnp.dot(key_t[part], grad_score, preferred_element_type=F32))
            key_add = jnp.dot(grad_score, query_h, preferred_element_type=F32)
            value_add = jnp.dot(weight, grad_h, preferred_element_type=F32)
            key_grad = key_add if key_grad is None else key_grad + key_add
            value_grad = value_add if value_grad is None else value_grad + value_add
        o_buf[g] = jnp.concatenate(attended_t, axis=0).T.astype(BF)
        dq_buf[g] = (jnp.concatenate(query_grad_t, axis=0) * (HD ** -0.5)).T.astype(BF)
        store(g, 0).start()
        store(g, 1).start()
        sums = jnp.concatenate([key_grad, value_grad], axis=1)
        centre[lax.rem(g, 3)] = sums[:CENTER]
        hret_out[g] = sums[CENTER:].astype(BF)
        for way in range(2):
            send(
                h_to[way], at_seam[way] & side_picked(g),
                lambda: [h_return(g, way)], lambda: [h_return_first(g, way)],
            )

    def send_rows(g):
        for way in range(2):
            @pl.when(h_from[way])
            def _():
                h_return(g, way).wait_recv()
        sums = centre[lax.rem(g, 3)] + jnp.dot(sel_t[...], hret_in[g], preferred_element_type=F32)
        own[g] = sums[STRIP : STRIP + OWN]
        vret_out[g, 0] = sums[:STRIP].astype(BF)
        vret_out[g, 1] = sums[STRIP + OWN :].astype(BF)
        for way in range(2):
            send(
                v_to[way], by_relay(g, way),
                lambda: [v_return(g, way)], lambda: [v_return_first(g, way)],
            )

    def hand_rows(g):
        for way, mine in ((0, jnp.logical_not(even_row)), (1, even_row)):
            @pl.when(mine & hands_on(g))
            def _():
                for copy in v_forward_first(g, way):
                    copy.wait_recv()
                for copy in v_forward_second(g, way):
                    copy.start()

    def hand_rows_back(g):
        for way, mine in ((0, jnp.logical_not(even_row)), (1, even_row)):
            @pl.when(mine & hands_on(g))
            def _():
                v_return_first(g, way).wait_recv()
                v_return_second(g, way).start()

    def hand_sides(g):
        for way in range(2):
            @pl.when(hands_sides(g, way))
            def _():
                h_forward_first(g, way).wait_recv()
                h_forward_second(g, way).start()

    def hand_sides_back(g):
        for way in range(2):
            @pl.when(hands_sides(g, way))
            def _():
                h_return_first(g, way).wait_recv()
                h_return_second(g, way).start()

    def step(i, carry):
        def stage(lag, work):
            @pl.when((i >= lag) & (i < groups + lag))
            def _():
                work(i - lag)

        for n in range(RATE):
            @pl.when(LEAD + RATE * i + n < groups)
            def _():
                start_rows(LEAD + RATE * i + n)

        stage(-1, hand_rows)
        stage(1, hand_sides)
        stage(0, send_sides)
        stage(3, attend)
        stage(4, hand_sides_back)
        stage(5, send_rows)
        stage(6, hand_rows_back)
        return carry

    hand_rows(0)
    lax.fori_loop(0, groups + 6, step, 0)

    def finish(g, carry):
        for way in range(2):
            @pl.when(v_from[way])
            def _():
                v_return(g, way).wait_recv()
        own[g, pl.ds(OWN - STRIP, STRIP), :] += vret_in[g, 0].astype(F32)
        own[g, pl.ds(0, STRIP), :] += vret_in[g, 1].astype(F32)
        dk_buf[g] = own[g, :, pl.ds(0, LANES)].astype(BF)
        dv_buf[g] = own[g, :, pl.ds(LANES, LANES)].astype(BF)
        store(g, 2).start()
        store(g, 3).start()
        return carry

    lax.fori_loop(0, groups, finish, 0)

    def drain(g, carry):
        for n in range(4):
            store(g, n).wait()
        for way in range(2):
            @pl.when(v_to[way])
            def _():
                for copy in v_forward(g, way):
                    copy.wait_send()
                v_return(g, way).wait_send()

            @pl.when(h_to[way])
            def _():
                h_forward(g, way).wait_send()
                h_return(g, way).wait_send()

        @pl.when(hands_on(g))
        def _():
            for copy in v_forward_second(g, 0):
                copy.wait_send()
            v_return_second(g, 0).wait_send()

        @pl.when(hands_sides(g, 0) | hands_sides(g, 1))
        def _():
            h_forward_second(g, 0).wait_send()
            h_return_second(g, 0).wait_send()

        return carry

    lax.fori_loop(0, groups, drain, 0)
    for way in range(2):
        @pl.when(v_to[way])
        def _():
            live_v(way).wait_send()

        @pl.when(h_to[way])
        def _():
            live_h(way).wait_send()


def write_out(*refs):
    ins, outs, bufs, sem = refs[:4], refs[4:8], refs[8:12], refs[12]
    reads = [pltpu.make_async_copy(a, b, sem.at[0, n]) for n, (a, b) in enumerate(zip(ins, bufs))]
    writes = [pltpu.make_async_copy(a, b, sem.at[1, n]) for n, (a, b) in enumerate(zip(bufs, outs))]
    for copy in reads:
        copy.start()
    for read, write in zip(reads, writes):
        read.wait()
        write.start()
    for copy in writes:
        copy.wait()


def per_device(queries, keys, values, out_grad, tissue):
    width = queries.shape[-1]
    groups = width // LANES
    flat = (OWN, width)
    any_spec = pl.BlockSpec(memory_space=pl.ANY)
    dma = pltpu.SemaphoreType.DMA
    outs = pl.pallas_call(
        functools.partial(kernel, groups, lax.axis_size("gx"), lax.axis_size("gy")),
        out_shape=[jax.ShapeDtypeStruct(flat, BF)] * 4,
        in_specs=[any_spec] * 4 + [pl.BlockSpec(memory_space=pltpu.VMEM)],
        out_specs=[any_spec] * 4,
        scratch_shapes=[
            pltpu.VMEM((groups, KEYS, 2 * LANES), BF),
            pltpu.VMEM((groups, OWN, LANES), BF),
            pltpu.VMEM((groups, OWN, LANES), BF),
            pltpu.VMEM((KEYS, LANES), BF),
            pltpu.VMEM((OWN, LANES), BF),
            pltpu.VMEM((2 * SLOTS, CENTER), BF),
            pltpu.VMEM((CENTER, 2 * SLOTS), BF),
            pltpu.VMEM((3, LANES, LANES), BF),
            pltpu.VMEM((16, LANES), F32),
            pltpu.VMEM((8, OWN), F32),
            pltpu.VMEM((groups, 2 * SLOTS, 2 * LANES), BF),
            pltpu.VMEM((3, CENTER, 2 * LANES), F32),
            pltpu.VMEM((groups, OWN, 2 * LANES), F32),
            pltpu.VMEM((groups, 2 * SLOTS, 2 * LANES), BF),
            pltpu.VMEM((groups, 2 * SLOTS, 2 * LANES), BF),
            pltpu.VMEM((groups, 2, STRIP, 2 * LANES), BF),
            pltpu.VMEM((groups, 2, STRIP, 2 * LANES), BF),
            pltpu.VMEM((groups, OWN, LANES), BF),
            pltpu.VMEM((groups, OWN, LANES), BF),
            pltpu.VMEM((groups, OWN, LANES), BF),
            pltpu.VMEM((groups, OWN, LANES), BF),
            pltpu.VMEM((groups, STRIP, 2 * LANES), BF),
            pltpu.VMEM((groups, STRIP, 2 * LANES), BF),
            pltpu.VMEM((groups, SLOTS, 2 * LANES), BF),
            pltpu.VMEM((groups, SLOTS, 2 * LANES), BF),
            dma((groups, 4)), dma((groups, 4)),
            dma((groups, 2, 2)), dma((groups, 2, 2)),
            dma((groups, 2)), dma((groups, 2)),
            dma((groups, 2)), dma((groups, 2)),
            dma((groups, 2)), dma((groups, 2)),
            dma((2,)), dma((2,)), dma((2,)), dma((2,)),
            dma((groups, 2)), dma((groups, 2)), dma((groups,)), dma((groups,)),
            dma((groups,)), dma((groups,)), dma((groups,)), dma((groups,)),
        ],
        compiler_params=pltpu.CompilerParams(
            collective_id=0, has_side_effects=True, vmem_limit_bytes=56 * 1024 * 1024
        ),
    )(
        keys.reshape(flat), values.reshape(flat), queries.reshape(flat), out_grad.reshape(flat),
        tissue,
    )
    outs = pl.pallas_call(
        write_out,
        out_shape=[jax.ShapeDtypeStruct(flat, BF)] * 4,
        in_specs=[any_spec] * 4,
        out_specs=[any_spec] * 4,
        scratch_shapes=[pltpu.VMEM(flat, BF)] * 4 + [dma((2, 4))],
    )(*outs)
    return tuple(out.reshape(queries.shape) for out in outs)


def solution(mesh):
    tokens = P("gy", "gx", None)
    return jax.shard_map(
        per_device, mesh=mesh, in_specs=(tokens,) * 4 + (P("gy", "gx"),),
        out_specs=(tokens,) * 4, check_vma=False,
    )
```

```python
import functools

import jax
import jax.numpy as jnp
from jax import lax
from jax.experimental import pallas as pl
from jax.experimental.pallas import tpu as pltpu
from jax.sharding import PartitionSpec as P

MESH = pl.DeviceIdType.MESH
HD = 64
RAD = 6
TH = 8
TW = 32
LANES = 128
OWN = TH * TW
STRIP = RAD * TW
CENTER = OWN + 2 * STRIP
SPAN = TH + 2 * RAD
SLOTS = 128
KEYS = CENTER + 2 * SLOTS
TOP = OWN - STRIP
SIDES = 3 * OWN
ROWS = SIDES + 2 * SLOTS
FAR = -1e30
LEAD = 3
RATE = 1
BF = jnp.bfloat16
F32 = jnp.float32


def iota(shape, dim):
    return lax.broadcasted_iota(jnp.int32, shape, dim)


def slot_row(slot):
    return jnp.floor((slot.astype(F32) + 0.5) * (1.0 / RAD)).astype(jnp.int32)


def select_rows(shape, slot_dim):
    slot_all, token = iota(shape, slot_dim), iota(shape, 1 - slot_dim)
    right = slot_all >= SLOTS
    slot = jnp.where(right, slot_all - SLOTS, slot_all)
    row = slot_row(slot)
    col = slot - row * RAD + jnp.where(right, TW - RAD, 0)
    hit = (slot < SPAN * RAD) & (token == row * TW + col)
    return jnp.where(hit, 1.0, 0.0).astype(BF)


def key_features(row, col, tile_col, padded, dead_tile):
    count = row.shape[0]
    lane = iota((count, LANES), 1)
    tile_row = jnp.where(
        row < RAD, 16 + TH - RAD + row, jnp.where(row < RAD + TH, row - RAD, 32 + row - RAD - TH)
    )
    pick = jnp.where(lane == tile_row, 1.0, 0.0).astype(BF)
    dead = jnp.dot(pick, dead_tile, preferred_element_type=F32)
    dead_part = jnp.where(lane == tile_col, dead, 0.0)
    row_part = jnp.where(jnp.abs(row - RAD - (lane - 32)) > RAD, 1.0, 0.0)
    col_part = jnp.where(jnp.abs(col - (lane - 40)) > RAD, 1.0, 0.0)
    pad_part = jnp.where((lane == 72) & padded, 1.0, 0.0)
    out = jnp.where(
        lane < 32, dead_part, jnp.where(lane < 40, row_part, jnp.where(lane < 72, col_part, pad_part))
    )
    return (out * FAR).astype(BF)


def kernel(
    groups, nx, ny,
    k_hbm, v_hbm, q_hbm, g_hbm, tissue_ref,
    o_hbm, dq_hbm, dk_hbm, dv_hbm,
    kv, q_buf, g_buf, feat, qfeat, sel, sel_t, dead, dead32, live_q,
    hsend, centre, own, part, hret_out, hret_in, xret_out, xret_in, zret_out, zret_in,
    o_buf, dq_buf, dk_buf, dv_buf,
    side_relay, side_relay_back,
    in_sem, out_sem, zf_send, zf_recv, xf_send, xf_recv, hf_send, hf_recv, hr_send, hr_recv,
    xr_send, xr_recv, zr_send, zr_recv,
    lv_send, lv_recv, lh_send, lh_recv,
    sf_send, sf_recv, sb_send, sb_recv,
):
    gx, gy = lax.axis_index("gx"), lax.axis_index("gy")
    has_up, has_down = gy > 0, gy < ny - 1
    has_left, has_right = gx > 0, gx < nx - 1
    up = (gx, jnp.maximum(gy - 1, 0))
    down = (gx, jnp.minimum(gy + 1, ny - 1))
    left = (jnp.maximum(gx - 1, 0), gy)
    right = (jnp.minimum(gx + 1, nx - 1), gy)
    odd = lax.rem(gy, 2)
    even_row = odd == 0
    partner = (gx, gy + 1 - 2 * odd)
    has_next = jnp.where(even_row, gy < ny - 2, gy >= 2)
    has_last = jnp.where(even_row, gy >= 2, gy < ny - 2)
    next_tile = (gx, jnp.clip(gy + 2 - 4 * odd, 0, ny - 1))
    last_tile = (gx, jnp.clip(gy - 2 + 4 * odd, 0, ny - 1))

    half = nx // 2
    seam = (gx == half - 1) | (gx == half)
    at_seam = ((gx == half), (gx == half - 1))
    routes = 3
    by_way = (tuple(2 * n for n in range(routes)), tuple(nx - 1 - 2 * n for n in range(routes)))

    def side_route(g):
        return jnp.where((g >= 1) & (g <= 6), 1 + lax.rem(g - 1, routes), 0)

    def relay_of(g, way):
        number = jnp.maximum(side_route(g) - 1, 0)
        return (2 * number if way == 0 else nx - 1 - 2 * number, gy)

    def side_picked(g):
        return side_route(g) > 0

    def hands_sides(g, way):
        return side_picked(g) & (gx == relay_of(g, way)[0])

    seam_to = ((half - 1, gy), (half, gy))
    on_route = (gx == by_way[0][0])
    for spot in by_way[0][1:] + by_way[1]:
        on_route = on_route | (gx == spot)

    sides = [
        (has_up, up), (has_down, down), (has_left, left), (has_right, right),
        (has_next, next_tile), (has_last, last_tile),
    ]
    sides += [(seam, (spot, gy)) for spot in by_way[0] + by_way[1]]
    sides += [(on_route, spot) for spot in seam_to]

    def lanes_of(g):
        return pl.ds(pl.multiple_of(g * LANES, LANES), LANES)

    def remote(src, dst, send, recv, where):
        return pltpu.make_async_remote_copy(
            src_ref=src, dst_ref=dst, send_sem=send, recv_sem=recv,
            device_id=where, device_id_type=MESH,
        )

    def loads(g):
        at = lanes_of(g)
        mid = pl.ds(OWN, OWN)
        return [
            pltpu.make_async_copy(k_hbm.at[:, at], kv.at[g, mid, pl.ds(0, LANES)], in_sem.at[g, 0]),
            pltpu.make_async_copy(v_hbm.at[:, at], kv.at[g, mid, pl.ds(LANES, LANES)], in_sem.at[g, 1]),
            pltpu.make_async_copy(q_hbm.at[:, at], q_buf.at[g], in_sem.at[g, 2]),
            pltpu.make_async_copy(g_hbm.at[:, at], g_buf.at[g], in_sem.at[g, 3]),
        ]

    def store(g, n):
        buf, hbm = ((o_buf, o_hbm), (dq_buf, dq_hbm), (dk_buf, dk_hbm), (dv_buf, dv_hbm))[n]
        return pltpu.make_async_copy(buf.at[g], hbm.at[:, lanes_of(g)], out_sem.at[g, n])

    def z_forward(g):
        to_rows = pl.ds(pl.multiple_of(odd * (2 * OWN), OWN), OWN)
        return [
            remote(
                hbm.at[:, lanes_of(g)], kv.at[g, to_rows, pl.ds(n * LANES, LANES)],
                zf_send.at[g, n], zf_recv.at[g, n], partner,
            )
            for n, hbm in enumerate((k_hbm, v_hbm))
        ]

    def x_forward(g):
        from_rows = pl.ds(pl.multiple_of((1 - odd) * (SIDES - STRIP), 64), STRIP)
        to_rows = pl.ds(pl.multiple_of(TOP + odd * (STRIP + OWN), 64), STRIP)
        return remote(kv.at[g, from_rows], kv.at[g, to_rows], xf_send.at[g], xf_recv.at[g], next_tile)

    def x_return(g):
        return remote(xret_out.at[g], xret_in.at[g], xr_send.at[g], xr_recv.at[g], last_tile)

    def z_return(g):
        return remote(zret_out.at[g], zret_in.at[g], zr_send.at[g], zr_recv.at[g], partner)

    def h_forward_first(g, way):
        return remote(
            hsend.at[g, pl.ds(way * SLOTS, SLOTS)], side_relay.at[g],
            hf_send.at[g, way], sf_recv.at[g], relay_of(g, way),
        )

    def h_forward_second(g, way):
        to_rows = pl.ds(SIDES + (1 - way) * SLOTS, SLOTS)
        return remote(
            side_relay.at[g], kv.at[g, to_rows], sf_send.at[g], hf_recv.at[g, way], seam_to[way],
        )

    def h_return_first(g, way):
        return remote(
            hret_out.at[g, pl.ds(way * SLOTS, SLOTS)], side_relay_back.at[g],
            hr_send.at[g, way], sb_recv.at[g], relay_of(g, way),
        )

    def h_return_second(g, way):
        return remote(
            side_relay_back.at[g], hret_in.at[g, pl.ds((1 - way) * SLOTS, SLOTS)],
            sb_send.at[g], hr_recv.at[g, way], seam_to[way],
        )

    def h_forward(g, way):
        to_rows = pl.ds(SIDES + (1 - way) * SLOTS, SLOTS)
        return remote(
            hsend.at[g, pl.ds(way * SLOTS, SLOTS)], kv.at[g, to_rows],
            hf_send.at[g, way], hf_recv.at[g, way], left if way == 0 else right,
        )

    def h_return(g, way):
        return remote(
            hret_out.at[g, pl.ds(way * SLOTS, SLOTS)], hret_in.at[g, pl.ds((1 - way) * SLOTS, SLOTS)],
            hr_send.at[g, way], hr_recv.at[g, way], left if way == 0 else right,
        )

    def live_v(way):
        to_rows = pl.ds(32, 16) if way == 0 else pl.ds(16, 16)
        return remote(
            dead.at[0, pl.ds(0, 16)], dead.at[0, to_rows],
            lv_send.at[way], lv_recv.at[way], up if way == 0 else down,
        )

    def live_h(way):
        return remote(
            dead.at[0, pl.ds(0, 48)], dead.at[2 - way, pl.ds(0, 48)],
            lh_send.at[way], lh_recv.at[way], left if way == 0 else right,
        )

    v_to = (has_up, has_down)
    v_from = (has_down, has_up)
    h_to = (has_left, has_right)
    h_from = (has_right, has_left)

    def send(here, special, direct, first):
        @pl.when(here & jnp.logical_not(special))
        def _():
            for copy in direct():
                copy.start()

        @pl.when(here & special)
        def _():
            for copy in first():
                copy.start()

    def start_rows(g):
        for copy in z_forward(g):
            copy.start()

    def start_loads(g, carry):
        for copy in loads(g):
            copy.start()
        return carry

    lax.fori_loop(0, groups, start_loads, 0)

    dead32[...] = jnp.ones_like(dead32)
    dead32[pl.ds(0, TH), pl.ds(0, TW)] = jnp.where(tissue_ref[...] > 0, 0.0, 1.0)
    dead[...] = jnp.zeros_like(dead)
    dead[0, pl.ds(0, 16), :] = dead32[...].astype(BF)
    for here, tile, first, count in (
        (has_up, 0, 16, 16), (has_down, 0, 32, 16), (has_left, 1, 0, 48), (has_right, 2, 0, 48),
    ):
        @pl.when(jnp.logical_not(here))
        def _():
            dead[tile, pl.ds(first, count), :] = jnp.ones((count, LANES), BF)

    for here, first, count in (
        (has_up, TOP, STRIP), (has_down, 2 * OWN, STRIP),
        (has_left, SIDES, SLOTS), (has_right, SIDES + SLOTS, SLOTS),
    ):
        @pl.when(jnp.logical_not(here))
        def _():
            def clear(g, carry):
                kv[g, pl.ds(first, count), :] = jnp.zeros((count, 2 * LANES), BF)
                return carry

            lax.fori_loop(0, groups, clear, 0)

    @pl.when(jnp.logical_not(has_next))
    def _():
        def clear(g, carry):
            xret_in[g] = jnp.zeros((STRIP, 2 * LANES), BF)
            return carry

        lax.fori_loop(0, groups, clear, 0)

    for here, first in ((has_left, 0), (has_right, SLOTS)):
        @pl.when(jnp.logical_not(here))
        def _():
            def clear(g, carry):
                hret_in[g, pl.ds(first, SLOTS), :] = jnp.zeros((SLOTS, 2 * LANES), BF)
                return carry

            lax.fori_loop(0, groups, clear, 0)

    barrier = pltpu.get_barrier_semaphore()
    for here, where in sides:
        @pl.when(here)
        def _():
            pl.semaphore_signal(barrier, inc=1, device_id=where, device_id_type=MESH)
    peers = sum(here.astype(jnp.int32) for here, _ in sides)
    pl.semaphore_wait(barrier, peers)

    for way in range(2):
        @pl.when(v_to[way])
        def _():
            live_v(way).start()

    def start_forward(g, carry):
        start_rows(g)
        return carry

    lax.fori_loop(0, LEAD, start_forward, 0)

    sel[...] = select_rows((2 * SLOTS, CENTER), 0)
    sel_t[...] = select_rows((CENTER, 2 * SLOTS), 1)
    token, lane = iota((OWN, LANES), 0), iota((OWN, LANES), 1)
    same = (
        (lane < 32)
        | ((lane >= 32) & (lane < 40) & (lane - 32 == token // TW))
        | ((lane >= 40) & (lane < 72) & (lane - 40 == token % TW))
        | (lane == 72)
    )
    qfeat[...] = jnp.where(same, 1.0, 0.0).astype(BF)

    for way in range(2):
        @pl.when(v_from[way])
        def _():
            live_v(way).wait_recv()
    for way in range(2):
        @pl.when(h_to[way])
        def _():
            live_h(way).start()

    tile = dead[0].astype(F32).T.astype(BF)
    row_of, token_of = iota((LANES, OWN), 0), iota((LANES, OWN), 1)
    pick = jnp.where(row_of == token_of // TW, 1.0, 0.0).astype(BF)
    spread = jnp.dot(tile, pick, preferred_element_type=F32)
    dead_q = jnp.sum(jnp.where(row_of == token_of % TW, spread, 0.0), axis=0, keepdims=True)
    live_q[...] = jnp.broadcast_to(1.0 - dead_q, (8, OWN))

    token = iota((CENTER, LANES), 0)
    feat[pl.ds(0, CENTER), :] = key_features(
        token // TW, token % TW, token % TW, token < 0, dead[0]
    )
    for way in range(2):
        @pl.when(h_from[way])
        def _():
            live_h(way).wait_recv()
    slot = iota((SLOTS, LANES), 0)
    row = slot_row(slot)
    col = slot - row * RAD
    none = slot >= SPAN * RAD
    feat[pl.ds(CENTER, SLOTS), :] = key_features(row, col - RAD, col + TW - RAD, none, dead[1])
    feat[pl.ds(CENTER + SLOTS, SLOTS), :] = key_features(row, col + TW, col, none, dead[2])

    def send_sides(g):
        for copy in loads(g):
            copy.wait()

        @pl.when(has_last)
        def _():
            x_forward(g).wait_recv()

        picked = jnp.dot(sel[...], kv[g, pl.ds(TOP, CENTER), :], preferred_element_type=F32)
        hsend[g] = picked.astype(BF)
        for way in range(2):
            send(
                h_to[way], at_seam[way] & side_picked(g),
                lambda: [h_forward(g, way)], lambda: [h_forward_first(g, way)],
            )

    def attend(g):
        for way in range(2):
            @pl.when(h_from[way])
            def _():
                h_forward(g, way).wait_recv()
        key_all, value_all = (
            jnp.concatenate(
                [kv[g, pl.ds(TOP, CENTER), pl.ds(n, LANES)], kv[g, pl.ds(SIDES, 2 * SLOTS), pl.ds(n, LANES)]],
                axis=0,
            )
            for n in (0, LANES)
        )
        key_t, value_t = key_all.T, value_all.T
        query = q_buf[g] * (HD ** -0.5)
        grad = g_buf[g]
        grad_t = grad.T.astype(F32)
        with_feat = jnp.concatenate([key_all, feat[...]], axis=1)
        head_of = iota((OWN, LANES), 1) // HD
        nothing = jnp.zeros((OWN, LANES), BF)
        live_row = live_q[pl.ds(0, 1), :]
        contract = (((1,), (1,)), ((), ()))
        parts = [slice(head * HD, (head + 1) * HD) for head in range(2)]
        queries_h = [jnp.where(head_of == head, query, nothing) for head in range(2)]
        grads_h = [jnp.where(head_of == head, grad, nothing) for head in range(2)]

        def scores_of(head):
            return lax.dot_general(
                with_feat, jnp.concatenate([queries_h[head], qfeat[...]], axis=1), contract,
                preferred_element_type=F32,
            )

        def attention_of(scores):
            top = jnp.max(scores, axis=0, keepdims=True)
            raised = jnp.exp(scores - top)
            total = jnp.sum(raised, axis=0, keepdims=True)
            return raised * (live_row / total)

        def attended_of(head, weight):
            out = jnp.dot(value_t[parts[head]], weight, preferred_element_type=F32)
            return out.astype(BF).astype(F32)

        def delta_of(head, out):
            return jnp.sum(out * grad_t[parts[head]], axis=0, keepdims=True)

        def grad_prob_of(head):
            return lax.dot_general(value_all, grads_h[head], contract, preferred_element_type=F32)

        def query_grad_of(head, grad_score):
            return jnp.dot(key_t[parts[head]], grad_score, preferred_element_type=F32)

        scores_0, scores_1 = scores_of(0), scores_of(1)
        attention_0 = attention_of(scores_0)
        weight_0 = attention_0.astype(BF)
        prob_0 = grad_prob_of(0)
        out_0 = attended_of(0, weight_0)
        attention_1 = attention_of(scores_1)
        weight_1 = attention_1.astype(BF)
        prob_1 = grad_prob_of(1)
        delta_0 = delta_of(0, out_0)
        out_1 = attended_of(1, weight_1)
        score_0 = (attention_0 * (prob_0 - delta_0)).astype(BF)
        delta_1 = delta_of(1, out_1)
        query_grad_0 = query_grad_of(0, score_0)
        score_1 = (attention_1 * (prob_1 - delta_1)).astype(BF)
        query_grad_1 = query_grad_of(1, score_1)
        key_grad = jnp.dot(
            jnp.concatenate([score_0, score_1], axis=1), jnp.concatenate(queries_h, axis=0),
            preferred_element_type=F32,
        )
        value_grad = jnp.dot(
            jnp.concatenate([weight_0, weight_1], axis=1), jnp.concatenate(grads_h, axis=0),
            preferred_element_type=F32,
        )
        o_buf[g] = jnp.concatenate([out_0, out_1], axis=0).T.astype(BF)
        dq_buf[g] = (jnp.concatenate([query_grad_0, query_grad_1], axis=0) * (HD ** -0.5)).T.astype(BF)
        store(g, 0).start()
        store(g, 1).start()
        sums = jnp.concatenate([key_grad, value_grad], axis=1)
        centre[lax.rem(g, 3)] = sums[:CENTER]
        hret_out[g] = sums[CENTER:].astype(BF)
        for way in range(2):
            send(
                h_to[way], at_seam[way] & side_picked(g),
                lambda: [h_return(g, way)], lambda: [h_return_first(g, way)],
            )

    def send_rows(g):
        for way in range(2):
            @pl.when(h_from[way])
            def _():
                h_return(g, way).wait_recv()
        sums = centre[lax.rem(g, 3)] + jnp.dot(sel_t[...], hret_in[g], preferred_element_type=F32)
        own[g] = sums[STRIP : STRIP + OWN]
        above, below = sums[:STRIP], sums[STRIP + OWN :]

        @pl.when(even_row)
        def _():
            xret_out[g] = above.astype(BF)
            part[g] = below

        @pl.when(jnp.logical_not(even_row))
        def _():
            xret_out[g] = below.astype(BF)
            part[g] = above

        @pl.when(has_last)
        def _():
            x_return(g).start()

    def send_partner(g):
        @pl.when(has_next)
        def _():
            x_return(g).wait_recv()

        mine, other = part[g], xret_in[g].astype(F32)
        first, second = jnp.where(even_row, mine, other), jnp.where(even_row, other, mine)
        cut, tail = OWN - STRIP, 2 * STRIP - OWN
        zret_out[g] = jnp.concatenate(
            [first[:cut], first[cut:] + second[:tail], second[tail:]], axis=0
        ).astype(BF)
        z_return(g).start()

    def hand_rows(g):
        for copy in z_forward(g):
            copy.wait_recv()

        @pl.when(has_next)
        def _():
            x_forward(g).start()

    def hand_sides(g):
        for way in range(2):
            @pl.when(hands_sides(g, way))
            def _():
                h_forward_first(g, way).wait_recv()
                h_forward_second(g, way).start()

    def hand_sides_back(g):
        for way in range(2):
            @pl.when(hands_sides(g, way))
            def _():
                h_return_first(g, way).wait_recv()
                h_return_second(g, way).start()

    def step(i, carry):
        def stage(lag, work):
            @pl.when((i >= lag) & (i < groups + lag))
            def _():
                work(i - lag)

        for n in range(RATE):
            @pl.when(LEAD + RATE * i + n < groups)
            def _():
                start_rows(LEAD + RATE * i + n)

        stage(-1, hand_rows)
        stage(1, hand_sides)
        stage(0, send_sides)
        stage(2, attend)
        stage(3, hand_sides_back)
        stage(4, send_rows)
        stage(5, send_partner)
        return carry

    hand_rows(0)
    lax.fori_loop(0, groups + 5, step, 0)

    def finish(g, carry):
        z_return(g).wait_recv()
        own[g] += zret_in[g].astype(F32)
        dk_buf[g] = own[g, :, pl.ds(0, LANES)].astype(BF)
        dv_buf[g] = own[g, :, pl.ds(LANES, LANES)].astype(BF)
        store(g, 2).start()
        store(g, 3).start()
        return carry

    lax.fori_loop(0, groups, finish, 0)

    def drain(g, carry):
        for n in range(4):
            store(g, n).wait()
        for copy in z_forward(g):
            copy.wait_send()
        z_return(g).wait_send()

        @pl.when(has_next)
        def _():
            x_forward(g).wait_send()

        @pl.when(has_last)
        def _():
            x_return(g).wait_send()

        for way in range(2):
            @pl.when(h_to[way])
            def _():
                h_forward(g, way).wait_send()
                h_return(g, way).wait_send()

        @pl.when(hands_sides(g, 0) | hands_sides(g, 1))
        def _():
            h_forward_second(g, 0).wait_send()
            h_return_second(g, 0).wait_send()

        return carry

    lax.fori_loop(0, groups, drain, 0)
    for way in range(2):
        @pl.when(v_to[way])
        def _():
            live_v(way).wait_send()

        @pl.when(h_to[way])
        def _():
            live_h(way).wait_send()


def write_out(*refs):
    ins, outs, bufs, sem = refs[:4], refs[4:8], refs[8:12], refs[12]
    reads = [pltpu.make_async_copy(a, b, sem.at[0, n]) for n, (a, b) in enumerate(zip(ins, bufs))]
    writes = [pltpu.make_async_copy(a, b, sem.at[1, n]) for n, (a, b) in enumerate(zip(bufs, outs))]
    for copy in reads:
        copy.start()
    for read, write in zip(reads, writes):
        read.wait()
        write.start()
    for copy in writes:
        copy.wait()


def per_device(queries, keys, values, out_grad, tissue):
    width = queries.shape[-1]
    groups = width // LANES
    flat = (OWN, width)
    any_spec = pl.BlockSpec(memory_space=pl.ANY)
    dma = pltpu.SemaphoreType.DMA
    outs = pl.pallas_call(
        functools.partial(kernel, groups, lax.axis_size("gx"), lax.axis_size("gy")),
        out_shape=[jax.ShapeDtypeStruct(flat, BF)] * 4,
        in_specs=[any_spec] * 4 + [pl.BlockSpec(memory_space=pltpu.VMEM)],
        out_specs=[any_spec] * 4,
        scratch_shapes=[
            pltpu.VMEM((groups, ROWS, 2 * LANES), BF),
            pltpu.VMEM((groups, OWN, LANES), BF),
            pltpu.VMEM((groups, OWN, LANES), BF),
            pltpu.VMEM((KEYS, LANES), BF),
            pltpu.VMEM((OWN, LANES), BF),
            pltpu.VMEM((2 * SLOTS, CENTER), BF),
            pltpu.VMEM((CENTER, 2 * SLOTS), BF),
            pltpu.VMEM((3, LANES, LANES), BF),
            pltpu.VMEM((16, LANES), F32),
            pltpu.VMEM((8, OWN), F32),
            pltpu.VMEM((groups, 2 * SLOTS, 2 * LANES), BF),
            pltpu.VMEM((3, CENTER, 2 * LANES), F32),
            pltpu.VMEM((groups, OWN, 2 * LANES), F32),
            pltpu.VMEM((groups, STRIP, 2 * LANES), F32),
            pltpu.VMEM((groups, 2 * SLOTS, 2 * LANES), BF),
            pltpu.VMEM((groups, 2 * SLOTS, 2 * LANES), BF),
            pltpu.VMEM((groups, STRIP, 2 * LANES), BF),
            pltpu.VMEM((groups, STRIP, 2 * LANES), BF),
            pltpu.VMEM((groups, OWN, 2 * LANES), BF),
            pltpu.VMEM((groups, OWN, 2 * LANES), BF),
            pltpu.VMEM((groups, OWN, LANES), BF),
            pltpu.VMEM((groups, OWN, LANES), BF),
            pltpu.VMEM((groups, OWN, LANES), BF),
            pltpu.VMEM((groups, OWN, LANES), BF),
            pltpu.VMEM((groups, SLOTS, 2 * LANES), BF),
            pltpu.VMEM((groups, SLOTS, 2 * LANES), BF),
            dma((groups, 4)), dma((groups, 4)),
            dma((groups, 2)), dma((groups, 2)), dma((groups,)), dma((groups,)),
            dma((groups, 2)), dma((groups, 2)), dma((groups, 2)), dma((groups, 2)),
            dma((groups,)), dma((groups,)), dma((groups,)), dma((groups,)),
            dma((2,)), dma((2,)), dma((2,)), dma((2,)),
            dma((groups,)), dma((groups,)), dma((groups,)), dma((groups,)),
        ],
        compiler_params=pltpu.CompilerParams(
            collective_id=0, has_side_effects=True, vmem_limit_bytes=56 * 1024 * 1024
        ),
    )(
        keys.reshape(flat), values.reshape(flat), queries.reshape(flat), out_grad.reshape(flat),
        tissue,
    )
    outs = pl.pallas_call(
        write_out,
        out_shape=[jax.ShapeDtypeStruct(flat, BF)] * 4,
        in_specs=[any_spec] * 4,
        out_specs=[any_spec] * 4,
        scratch_shapes=[pltpu.VMEM(flat, BF)] * 4 + [dma((2, 4))],
    )(*outs)
    return tuple(out.reshape(queries.shape) for out in outs)


def solution(mesh):
    tokens = P("gy", "gx", None)
    return jax.shard_map(
        per_device, mesh=mesh, in_specs=(tokens,) * 4 + (P("gy", "gx"),),
        out_specs=(tokens,) * 4, check_vma=False,
    )
```

```python
import functools

import jax
import jax.numpy as jnp
from jax import lax
from jax.experimental import pallas as pl
from jax.experimental.pallas import tpu as pltpu
from jax.sharding import PartitionSpec as P

MESH = pl.DeviceIdType.MESH
HD = 64
RAD = 6
TH = 8
TW = 32
LANES = 128
OWN = TH * TW
STRIP = RAD * TW
CENTER = OWN + 2 * STRIP
SPAN = TH + 2 * RAD
SLOTS = 128
KEYS = CENTER + 2 * SLOTS
TOP = OWN - STRIP
SIDES = 3 * OWN
ROWS = SIDES + 2 * SLOTS
HALF = OWN // 2
REACH = HALF + 2 * STRIP
FAR = -1e30
LEAD = 3
RATE = 1
BF = jnp.bfloat16
F32 = jnp.float32


def iota(shape, dim):
    return lax.broadcasted_iota(jnp.int32, shape, dim)


def slot_row(slot):
    return jnp.floor((slot.astype(F32) + 0.5) * (1.0 / RAD)).astype(jnp.int32)


def select_rows(shape, slot_dim):
    slot_all, token = iota(shape, slot_dim), iota(shape, 1 - slot_dim)
    right = slot_all >= SLOTS
    slot = jnp.where(right, slot_all - SLOTS, slot_all)
    row = slot_row(slot)
    col = slot - row * RAD + jnp.where(right, TW - RAD, 0)
    hit = (slot < SPAN * RAD) & (token == row * TW + col)
    return jnp.where(hit, 1.0, 0.0).astype(BF)


def key_features(row, col, tile_col, padded, dead_tile):
    count = row.shape[0]
    lane = iota((count, LANES), 1)
    tile_row = jnp.where(
        row < RAD, 16 + TH - RAD + row, jnp.where(row < RAD + TH, row - RAD, 32 + row - RAD - TH)
    )
    pick = jnp.where(lane == tile_row, 1.0, 0.0).astype(BF)
    dead = jnp.dot(pick, dead_tile, preferred_element_type=F32)
    dead_part = jnp.where(lane == tile_col, dead, 0.0)
    row_part = jnp.where(jnp.abs(row - RAD - (lane - 32)) > RAD, 1.0, 0.0)
    col_part = jnp.where(jnp.abs(col - (lane - 40)) > RAD, 1.0, 0.0)
    pad_part = jnp.where((lane == 72) & padded, 1.0, 0.0)
    out = jnp.where(
        lane < 32, dead_part, jnp.where(lane < 40, row_part, jnp.where(lane < 72, col_part, pad_part))
    )
    return (out * FAR).astype(BF)


def kernel(
    groups, nx, ny,
    k_hbm, v_hbm, q_hbm, g_hbm, tissue_ref,
    o_hbm, dq_hbm, dk_hbm, dv_hbm,
    kv, q_buf, g_buf, feat, qfeat, sel, sel_t, dead, dead32, live_q,
    hsend, centre, own, part, hret_out, hret_in, xret_out, xret_in, zret_out, zret_in,
    o_buf, dq_buf, dk_buf, dv_buf,
    side_relay, side_relay_back,
    in_sem, out_sem, zf_send, zf_recv, xf_send, xf_recv, hf_send, hf_recv, hr_send, hr_recv,
    xr_send, xr_recv, zr_send, zr_recv,
    lv_send, lv_recv, lh_send, lh_recv,
    sf_send, sf_recv, sb_send, sb_recv,
):
    gx, gy = lax.axis_index("gx"), lax.axis_index("gy")
    has_up, has_down = gy > 0, gy < ny - 1
    has_left, has_right = gx > 0, gx < nx - 1
    up = (gx, jnp.maximum(gy - 1, 0))
    down = (gx, jnp.minimum(gy + 1, ny - 1))
    left = (jnp.maximum(gx - 1, 0), gy)
    right = (jnp.minimum(gx + 1, nx - 1), gy)
    odd = lax.rem(gy, 2)
    even_row = odd == 0
    partner = (gx, gy + 1 - 2 * odd)
    has_next = jnp.where(even_row, gy < ny - 2, gy >= 2)
    has_last = jnp.where(even_row, gy >= 2, gy < ny - 2)
    next_tile = (gx, jnp.clip(gy + 2 - 4 * odd, 0, ny - 1))
    last_tile = (gx, jnp.clip(gy - 2 + 4 * odd, 0, ny - 1))

    half = nx // 2
    seam = (gx == half - 1) | (gx == half)
    at_seam = ((gx == half), (gx == half - 1))
    routes = 3
    by_way = (tuple(2 * n for n in range(routes)), tuple(nx - 1 - 2 * n for n in range(routes)))

    def side_route(g):
        return jnp.where((g >= 1) & (g <= 6), 1 + lax.rem(g - 1, routes), 0)

    def relay_of(g, way):
        number = jnp.maximum(side_route(g) - 1, 0)
        return (2 * number if way == 0 else nx - 1 - 2 * number, gy)

    def side_picked(g):
        return side_route(g) > 0

    def hands_sides(g, way):
        return side_picked(g) & (gx == relay_of(g, way)[0])

    seam_to = ((half - 1, gy), (half, gy))
    on_route = (gx == by_way[0][0])
    for spot in by_way[0][1:] + by_way[1]:
        on_route = on_route | (gx == spot)

    sides = [
        (has_up, up), (has_down, down), (has_left, left), (has_right, right),
        (has_next, next_tile), (has_last, last_tile),
    ]
    sides += [(seam, (spot, gy)) for spot in by_way[0] + by_way[1]]
    sides += [(on_route, spot) for spot in seam_to]

    def lanes_of(g):
        return pl.ds(pl.multiple_of(g * LANES, LANES), LANES)

    def remote(src, dst, send, recv, where):
        return pltpu.make_async_remote_copy(
            src_ref=src, dst_ref=dst, send_sem=send, recv_sem=recv,
            device_id=where, device_id_type=MESH,
        )

    def loads(g):
        at = lanes_of(g)
        mid = pl.ds(OWN, OWN)
        return [
            pltpu.make_async_copy(k_hbm.at[:, at], kv.at[g, mid, pl.ds(0, LANES)], in_sem.at[g, 0]),
            pltpu.make_async_copy(v_hbm.at[:, at], kv.at[g, mid, pl.ds(LANES, LANES)], in_sem.at[g, 1]),
            pltpu.make_async_copy(q_hbm.at[:, at], q_buf.at[g], in_sem.at[g, 2]),
            pltpu.make_async_copy(g_hbm.at[:, at], g_buf.at[g], in_sem.at[g, 3]),
        ]

    def store(g, n):
        buf, hbm = ((o_buf, o_hbm), (dq_buf, dq_hbm), (dk_buf, dk_hbm), (dv_buf, dv_hbm))[n]
        return pltpu.make_async_copy(buf.at[g], hbm.at[:, lanes_of(g)], out_sem.at[g, n])

    def z_forward(g):
        to_rows = pl.ds(pl.multiple_of(odd * (2 * OWN), OWN), OWN)
        return [
            remote(
                hbm.at[:, lanes_of(g)], kv.at[g, to_rows, pl.ds(n * LANES, LANES)],
                zf_send.at[g, n], zf_recv.at[g, n], partner,
            )
            for n, hbm in enumerate((k_hbm, v_hbm))
        ]

    def x_forward(g):
        from_rows = pl.ds(pl.multiple_of((1 - odd) * (SIDES - STRIP), 64), STRIP)
        to_rows = pl.ds(pl.multiple_of(TOP + odd * (STRIP + OWN), 64), STRIP)
        return remote(kv.at[g, from_rows], kv.at[g, to_rows], xf_send.at[g], xf_recv.at[g], next_tile)

    def x_return(g):
        return remote(xret_out.at[g], xret_in.at[g], xr_send.at[g], xr_recv.at[g], last_tile)

    def z_return(g):
        return remote(zret_out.at[g], zret_in.at[g], zr_send.at[g], zr_recv.at[g], partner)

    def h_forward_first(g, way):
        return remote(
            hsend.at[g, pl.ds(way * SLOTS, SLOTS)], side_relay.at[g],
            hf_send.at[g, way], sf_recv.at[g], relay_of(g, way),
        )

    def h_forward_second(g, way):
        to_rows = pl.ds(SIDES + (1 - way) * SLOTS, SLOTS)
        return remote(
            side_relay.at[g], kv.at[g, to_rows], sf_send.at[g], hf_recv.at[g, way], seam_to[way],
        )

    def h_return_first(g, way):
        return remote(
            hret_out.at[g, pl.ds(way * SLOTS, SLOTS)], side_relay_back.at[g],
            hr_send.at[g, way], sb_recv.at[g], relay_of(g, way),
        )

    def h_return_second(g, way):
        return remote(
            side_relay_back.at[g], hret_in.at[g, pl.ds((1 - way) * SLOTS, SLOTS)],
            sb_send.at[g], hr_recv.at[g, way], seam_to[way],
        )

    def h_forward(g, way):
        to_rows = pl.ds(SIDES + (1 - way) * SLOTS, SLOTS)
        return remote(
            hsend.at[g, pl.ds(way * SLOTS, SLOTS)], kv.at[g, to_rows],
            hf_send.at[g, way], hf_recv.at[g, way], left if way == 0 else right,
        )

    def h_return(g, way):
        return remote(
            hret_out.at[g, pl.ds(way * SLOTS, SLOTS)], hret_in.at[g, pl.ds((1 - way) * SLOTS, SLOTS)],
            hr_send.at[g, way], hr_recv.at[g, way], left if way == 0 else right,
        )

    def live_v(way):
        to_rows = pl.ds(32, 16) if way == 0 else pl.ds(16, 16)
        return remote(
            dead.at[0, pl.ds(0, 16)], dead.at[0, to_rows],
            lv_send.at[way], lv_recv.at[way], up if way == 0 else down,
        )

    def live_h(way):
        return remote(
            dead.at[0, pl.ds(0, 48)], dead.at[2 - way, pl.ds(0, 48)],
            lh_send.at[way], lh_recv.at[way], left if way == 0 else right,
        )

    v_to = (has_up, has_down)
    v_from = (has_down, has_up)
    h_to = (has_left, has_right)
    h_from = (has_right, has_left)

    def send(here, special, direct, first):
        @pl.when(here & jnp.logical_not(special))
        def _():
            for copy in direct():
                copy.start()

        @pl.when(here & special)
        def _():
            for copy in first():
                copy.start()

    def start_rows(g):
        for copy in z_forward(g):
            copy.start()

    dead32[...] = jnp.ones_like(dead32)
    dead32[pl.ds(0, TH), pl.ds(0, TW)] = jnp.where(tissue_ref[...] > 0, 0.0, 1.0)
    dead[...] = jnp.zeros_like(dead)
    dead[0, pl.ds(0, 16), :] = dead32[...].astype(BF)
    for here, tile, first, count in (
        (has_up, 0, 16, 16), (has_down, 0, 32, 16), (has_left, 1, 0, 48), (has_right, 2, 0, 48),
    ):
        @pl.when(jnp.logical_not(here))
        def _():
            dead[tile, pl.ds(first, count), :] = jnp.ones((count, LANES), BF)

    barrier = pltpu.get_barrier_semaphore()
    for here, where in sides:
        @pl.when(here)
        def _():
            pl.semaphore_signal(barrier, inc=1, device_id=where, device_id_type=MESH)
    def start_loads(g, carry):
        for copy in loads(g):
            copy.start()
        return carry

    lax.fori_loop(0, groups, start_loads, 0)

    for here, first, count in (
        (has_up, TOP, STRIP), (has_down, 2 * OWN, STRIP),
        (has_left, SIDES, SLOTS), (has_right, SIDES + SLOTS, SLOTS),
    ):
        @pl.when(jnp.logical_not(here))
        def _():
            def clear(g, carry):
                kv[g, pl.ds(first, count), :] = jnp.zeros((count, 2 * LANES), BF)
                return carry

            lax.fori_loop(0, groups, clear, 0)

    @pl.when(jnp.logical_not(has_next))
    def _():
        def clear(g, carry):
            xret_in[g] = jnp.zeros((STRIP, 2 * LANES), BF)
            return carry

        lax.fori_loop(0, groups, clear, 0)

    for here, first in ((has_left, 0), (has_right, SLOTS)):
        @pl.when(jnp.logical_not(here))
        def _():
            def clear(g, carry):
                hret_in[g, pl.ds(first, SLOTS), :] = jnp.zeros((SLOTS, 2 * LANES), BF)
                return carry

            lax.fori_loop(0, groups, clear, 0)

    peers = sum(here.astype(jnp.int32) for here, _ in sides)
    pl.semaphore_wait(barrier, peers)

    for way in range(2):
        @pl.when(v_to[way])
        def _():
            live_v(way).start()

    def start_forward(g, carry):
        start_rows(g)
        return carry

    lax.fori_loop(0, LEAD, start_forward, 0)

    sel[...] = select_rows((2 * SLOTS, CENTER), 0)
    sel_t[...] = select_rows((CENTER, 2 * SLOTS), 1)
    token, lane = iota((OWN, LANES), 0), iota((OWN, LANES), 1)
    same = (
        (lane < 32)
        | ((lane >= 32) & (lane < 40) & (lane - 32 == token // TW))
        | ((lane >= 40) & (lane < 72) & (lane - 40 == token % TW))
        | (lane == 72)
    )
    qfeat[...] = jnp.where(same, 1.0, 0.0).astype(BF)

    for way in range(2):
        @pl.when(v_from[way])
        def _():
            live_v(way).wait_recv()
    for way in range(2):
        @pl.when(h_to[way])
        def _():
            live_h(way).start()

    tile = dead[0].astype(F32).T.astype(BF)
    row_of, token_of = iota((LANES, OWN), 0), iota((LANES, OWN), 1)
    pick = jnp.where(row_of == token_of // TW, 1.0, 0.0).astype(BF)
    spread = jnp.dot(tile, pick, preferred_element_type=F32)
    dead_q = jnp.sum(jnp.where(row_of == token_of % TW, spread, 0.0), axis=0, keepdims=True)
    live_q[...] = jnp.broadcast_to(1.0 - dead_q, (8, OWN))

    token = iota((CENTER, LANES), 0)
    feat[pl.ds(0, CENTER), :] = key_features(
        token // TW, token % TW, token % TW, token < 0, dead[0]
    )
    for way in range(2):
        @pl.when(h_from[way])
        def _():
            live_h(way).wait_recv()
    slot = iota((SLOTS, LANES), 0)
    row = slot_row(slot)
    col = slot - row * RAD
    none = slot >= SPAN * RAD
    feat[pl.ds(CENTER, SLOTS), :] = key_features(row, col - RAD, col + TW - RAD, none, dead[1])
    feat[pl.ds(CENTER + SLOTS, SLOTS), :] = key_features(row, col + TW, col, none, dead[2])

    def send_sides(g):
        for copy in loads(g):
            copy.wait()

        @pl.when(has_last)
        def _():
            x_forward(g).wait_recv()

        picked = jnp.dot(sel[...], kv[g, pl.ds(TOP, CENTER), :], preferred_element_type=F32)
        hsend[g] = picked.astype(BF)
        for way in range(2):
            send(
                h_to[way], at_seam[way] & side_picked(g),
                lambda: [h_forward(g, way)], lambda: [h_forward_first(g, way)],
            )

    def attend(g):
        for way in range(2):
            @pl.when(h_from[way])
            def _():
                h_forward(g, way).wait_recv()
        contract = (((1,), (1,)), ((), ()))
        query = q_buf[g] * (HD ** -0.5)
        grad = g_buf[g]
        head_of = iota((OWN, LANES), 1) // HD
        nothing = jnp.zeros((OWN, LANES), BF)
        queries_h = [jnp.where(head_of == head, query, nothing) for head in range(2)]
        grads_h = [jnp.where(head_of == head, grad, nothing) for head in range(2)]
        grad_t = grad.T.astype(F32)
        side_keys, side_values = (kv[g, pl.ds(SIDES, 2 * SLOTS), pl.ds(n, LANES)] for n in (0, LANES))
        mid_keys, mid_values = (kv[g, pl.ds(TOP, CENTER), pl.ds(n, LANES)] for n in (0, LANES))
        side_keys_t, side_values_t = side_keys.T, side_values.T
        mid_keys_t, mid_values_t = mid_keys.T, mid_values.T

        def tokens_of(half):
            return slice(half * HALF, (half + 1) * HALF)

        def reach_of(half):
            return slice(half * HALF, half * HALF + REACH)

        def both(pair, half):
            return jnp.concatenate([x[tokens_of(half)] for x in pair], axis=0)

        def keys_of(half, mid, side):
            return jnp.concatenate([mid[reach_of(half)], side], axis=0)

        def keys_t_of(half, mid, side):
            return jnp.concatenate([mid[:, reach_of(half)], side], axis=1)

        def scores_of(half):
            feats = keys_of(half, feat[pl.ds(0, CENTER), :], feat[pl.ds(CENTER, 2 * SLOTS), :])
            own_feats = qfeat[pl.ds(half * HALF, HALF), :]
            return lax.dot_general(
                jnp.concatenate([keys_of(half, mid_keys, side_keys), feats], axis=1),
                jnp.concatenate(
                    [both(queries_h, half), jnp.concatenate([own_feats, own_feats], axis=0)], axis=1
                ),
                contract, preferred_element_type=F32,
            )

        def attention_of(half, scores):
            live = live_q[pl.ds(0, 1), pl.ds(half * HALF, HALF)]
            top = jnp.max(scores, axis=0, keepdims=True)
            raised = jnp.exp(scores - top)
            total = jnp.sum(raised, axis=0, keepdims=True)
            return raised * (jnp.concatenate([live, live], axis=1) / total)

        def per_head(out):
            return jnp.concatenate([out[:HD, :HALF], out[HD:, HALF:]], axis=0)

        def attended_of(half, weight):
            out = jnp.dot(
                keys_t_of(half, mid_values_t, side_values_t), weight, preferred_element_type=F32
            )
            return per_head(out).astype(BF).astype(F32)

        def delta_of(half, out):
            terms = out * grad_t[:, tokens_of(half)]
            return jnp.concatenate(
                [jnp.sum(terms[:HD], axis=0, keepdims=True), jnp.sum(terms[HD:], axis=0, keepdims=True)], axis=1
            )

        def grad_prob_of(half):
            return lax.dot_general(
                keys_of(half, mid_values, side_values), both(grads_h, half), contract,
                preferred_element_type=F32,
            )

        def query_grad_of(half, grad_score):
            return per_head(
                jnp.dot(keys_t_of(half, mid_keys_t, side_keys_t), grad_score, preferred_element_type=F32)
            )

        scores_0, scores_1 = scores_of(0), scores_of(1)
        attention_0 = attention_of(0, scores_0)
        weight_0 = attention_0.astype(BF)
        prob_0 = grad_prob_of(0)
        out_0 = attended_of(0, weight_0)
        attention_1 = attention_of(1, scores_1)
        weight_1 = attention_1.astype(BF)
        prob_1 = grad_prob_of(1)
        delta_0 = delta_of(0, out_0)
        out_1 = attended_of(1, weight_1)
        score_0 = (attention_0 * (prob_0 - delta_0)).astype(BF)
        delta_1 = delta_of(1, out_1)
        query_grad_0 = query_grad_of(0, score_0)
        score_1 = (attention_1 * (prob_1 - delta_1)).astype(BF)
        query_grad_1 = query_grad_of(1, score_1)

        def key_sums(factors, rows_h):
            first, second = (
                jnp.dot(factor, both(rows_h, half), preferred_element_type=F32)
                for half, factor in enumerate(factors)
            )
            middle = first[HALF:REACH] + second[: REACH - HALF]
            mid = jnp.concatenate([first[:HALF], middle, second[REACH - HALF : REACH]], axis=0)
            return mid, first[REACH:] + second[REACH:]

        key_mid, key_side = key_sums((score_0, score_1), queries_h)
        value_mid, value_side = key_sums((weight_0, weight_1), grads_h)
        o_buf[g] = jnp.concatenate([out_0, out_1], axis=1).T.astype(BF)
        dq_buf[g] = (jnp.concatenate([query_grad_0, query_grad_1], axis=1) * (HD ** -0.5)).T.astype(BF)
        store(g, 0).start()
        store(g, 1).start()
        centre[lax.rem(g, 3)] = jnp.concatenate([key_mid, value_mid], axis=1)
        hret_out[g] = jnp.concatenate([key_side, value_side], axis=1).astype(BF)
        for way in range(2):
            send(
                h_to[way], at_seam[way] & side_picked(g),
                lambda: [h_return(g, way)], lambda: [h_return_first(g, way)],
            )

    def send_rows(g):
        for way in range(2):
            @pl.when(h_from[way])
            def _():
                h_return(g, way).wait_recv()
        sums = centre[lax.rem(g, 3)] + jnp.dot(sel_t[...], hret_in[g], preferred_element_type=F32)
        own[g] = sums[STRIP : STRIP + OWN]
        above, below = sums[:STRIP], sums[STRIP + OWN :]

        @pl.when(even_row)
        def _():
            xret_out[g] = above.astype(BF)
            part[g] = below

        @pl.when(jnp.logical_not(even_row))
        def _():
            xret_out[g] = below.astype(BF)
            part[g] = above

        @pl.when(has_last)
        def _():
            x_return(g).start()

    def send_partner(g):
        @pl.when(has_next)
        def _():
            x_return(g).wait_recv()

        mine, other = part[g], xret_in[g].astype(F32)
        first, second = jnp.where(even_row, mine, other), jnp.where(even_row, other, mine)
        cut, tail = OWN - STRIP, 2 * STRIP - OWN
        zret_out[g] = jnp.concatenate(
            [first[:cut], first[cut:] + second[:tail], second[tail:]], axis=0
        ).astype(BF)
        z_return(g).start()

    def hand_rows(g):
        for copy in z_forward(g):
            copy.wait_recv()

        @pl.when(has_next)
        def _():
            x_forward(g).start()

    def hand_sides(g):
        for way in range(2):
            @pl.when(hands_sides(g, way))
            def _():
                h_forward_first(g, way).wait_recv()
                h_forward_second(g, way).start()

    def hand_sides_back(g):
        for way in range(2):
            @pl.when(hands_sides(g, way))
            def _():
                h_return_first(g, way).wait_recv()
                h_return_second(g, way).start()

    def step(i, carry):
        def stage(lag, work):
            @pl.when((i >= lag) & (i < groups + lag))
            def _():
                work(i - lag)

        for n in range(RATE):
            @pl.when(LEAD + RATE * i + n < groups)
            def _():
                start_rows(LEAD + RATE * i + n)

        stage(-1, hand_rows)
        stage(1, hand_sides)
        stage(0, send_sides)
        stage(2, attend)
        stage(3, hand_sides_back)
        stage(4, send_rows)
        stage(5, send_partner)
        return carry

    hand_rows(0)
    lax.fori_loop(0, groups + 5, step, 0)

    def drain(g, carry):
        store(g, 0).wait()
        store(g, 1).wait()
        for copy in z_forward(g):
            copy.wait_send()

        @pl.when(has_next)
        def _():
            x_forward(g).wait_send()

        @pl.when(has_last)
        def _():
            x_return(g).wait_send()

        for way in range(2):
            @pl.when(h_to[way])
            def _():
                h_forward(g, way).wait_send()
                h_return(g, way).wait_send()

        @pl.when(hands_sides(g, 0) | hands_sides(g, 1))
        def _():
            h_forward_second(g, 0).wait_send()
            h_return_second(g, 0).wait_send()

        return carry

    lax.fori_loop(0, groups, drain, 0)
    for way in range(2):
        @pl.when(v_to[way])
        def _():
            live_v(way).wait_send()

        @pl.when(h_to[way])
        def _():
            live_h(way).wait_send()

    def finish(g, carry):
        z_return(g).wait_recv()
        total = own[g] + zret_in[g].astype(F32)
        dk_buf[g] = total[:, :LANES].astype(BF)
        dv_buf[g] = total[:, LANES:].astype(BF)
        store(g, 2).start()
        store(g, 3).start()
        return carry

    lax.fori_loop(0, groups, finish, 0)

    def drain_last(g, carry):
        z_return(g).wait_send()
        store(g, 2).wait()
        store(g, 3).wait()
        return carry

    lax.fori_loop(0, groups, drain_last, 0)


def write_out(*refs):
    ins, outs, bufs, sem = refs[:4], refs[4:8], refs[8:12], refs[12]
    reads = [pltpu.make_async_copy(a, b, sem.at[0, n]) for n, (a, b) in enumerate(zip(ins, bufs))]
    writes = [pltpu.make_async_copy(a, b, sem.at[1, n]) for n, (a, b) in enumerate(zip(bufs, outs))]
    for copy in reads:
        copy.start()
    for read, write in zip(reads, writes):
        read.wait()
        write.start()
    for copy in writes:
        copy.wait()


def per_device(queries, keys, values, out_grad, tissue):
    width = queries.shape[-1]
    groups = width // LANES
    flat = (OWN, width)
    any_spec = pl.BlockSpec(memory_space=pl.ANY)
    dma = pltpu.SemaphoreType.DMA
    outs = pl.pallas_call(
        functools.partial(kernel, groups, lax.axis_size("gx"), lax.axis_size("gy")),
        out_shape=[jax.ShapeDtypeStruct(flat, BF)] * 4,
        in_specs=[any_spec] * 4 + [pl.BlockSpec(memory_space=pltpu.VMEM)],
        out_specs=[any_spec] * 4,
        scratch_shapes=[
            pltpu.VMEM((groups, ROWS, 2 * LANES), BF),
            pltpu.VMEM((groups, OWN, LANES), BF),
            pltpu.VMEM((groups, OWN, LANES), BF),
            pltpu.VMEM((KEYS, LANES), BF),
            pltpu.VMEM((OWN, LANES), BF),
            pltpu.VMEM((2 * SLOTS, CENTER), BF),
            pltpu.VMEM((CENTER, 2 * SLOTS), BF),
            pltpu.VMEM((3, LANES, LANES), BF),
            pltpu.VMEM((16, LANES), F32),
            pltpu.VMEM((8, OWN), F32),
            pltpu.VMEM((groups, 2 * SLOTS, 2 * LANES), BF),
            pltpu.VMEM((3, CENTER, 2 * LANES), F32),
            pltpu.VMEM((groups, OWN, 2 * LANES), F32),
            pltpu.VMEM((groups, STRIP, 2 * LANES), F32),
            pltpu.VMEM((groups, 2 * SLOTS, 2 * LANES), BF),
            pltpu.VMEM((groups, 2 * SLOTS, 2 * LANES), BF),
            pltpu.VMEM((groups, STRIP, 2 * LANES), BF),
            pltpu.VMEM((groups, STRIP, 2 * LANES), BF),
            pltpu.VMEM((groups, OWN, 2 * LANES), BF),
            pltpu.VMEM((groups, OWN, 2 * LANES), BF),
            pltpu.VMEM((groups, OWN, LANES), BF),
            pltpu.VMEM((groups, OWN, LANES), BF),
            pltpu.VMEM((groups, OWN, LANES), BF),
            pltpu.VMEM((groups, OWN, LANES), BF),
            pltpu.VMEM((groups, SLOTS, 2 * LANES), BF),
            pltpu.VMEM((groups, SLOTS, 2 * LANES), BF),
            dma((groups, 4)), dma((groups, 4)),
            dma((groups, 2)), dma((groups, 2)), dma((groups,)), dma((groups,)),
            dma((groups, 2)), dma((groups, 2)), dma((groups, 2)), dma((groups, 2)),
            dma((groups,)), dma((groups,)), dma((groups,)), dma((groups,)),
            dma((2,)), dma((2,)), dma((2,)), dma((2,)),
            dma((groups,)), dma((groups,)), dma((groups,)), dma((groups,)),
        ],
        compiler_params=pltpu.CompilerParams(
            collective_id=0, has_side_effects=True, vmem_limit_bytes=56 * 1024 * 1024
        ),
    )(
        keys.reshape(flat), values.reshape(flat), queries.reshape(flat), out_grad.reshape(flat),
        tissue,
    )
    outs = pl.pallas_call(
        write_out,
        out_shape=[jax.ShapeDtypeStruct(flat, BF)] * 4,
        in_specs=[any_spec] * 4,
        out_specs=[any_spec] * 4,
        scratch_shapes=[pltpu.VMEM(flat, BF)] * 4 + [dma((2, 4))],
    )(*outs)
    return tuple(out.reshape(queries.shape) for out in outs)


def solution(mesh):
    tokens = P("gy", "gx", None)
    return jax.shard_map(
        per_device, mesh=mesh, in_specs=(tokens,) * 4 + (P("gy", "gx"),),
        out_specs=(tokens,) * 4, check_vma=False,
    )
```

```python
import functools

import jax
import jax.numpy as jnp
from jax import lax
from jax.experimental import pallas as pl
from jax.experimental.pallas import tpu as pltpu
from jax.sharding import PartitionSpec as P

MESH = pl.DeviceIdType.MESH
HD = 64
RAD = 6
TH = 8
TW = 32
LANES = 128
OWN = TH * TW
STRIP = RAD * TW
CENTER = OWN + 2 * STRIP
SPAN = TH + 2 * RAD
SLOTS = 128
KEYS = CENTER + 2 * SLOTS
TOP = OWN - STRIP
SIDES = 3 * OWN
ROWS = SIDES + 2 * SLOTS
HALF = OWN // 2
REACH = HALF + 2 * STRIP
FAR = -1e30
LEAD = 3
RATE = 1
BF = jnp.bfloat16
F32 = jnp.float32


def iota(shape, dim):
    return lax.broadcasted_iota(jnp.int32, shape, dim)


def slot_row(slot):
    return jnp.floor((slot.astype(F32) + 0.5) * (1.0 / RAD)).astype(jnp.int32)


def select_rows(shape, slot_dim):
    slot_all, token = iota(shape, slot_dim), iota(shape, 1 - slot_dim)
    right = slot_all >= SLOTS
    slot = jnp.where(right, slot_all - SLOTS, slot_all)
    row = slot_row(slot)
    col = slot - row * RAD + jnp.where(right, TW - RAD, 0)
    hit = (slot < SPAN * RAD) & (token == row * TW + col)
    return jnp.where(hit, 1.0, 0.0).astype(BF)


def key_features(row, col, tile_col, padded, dead_tile):
    count = row.shape[0]
    lane = iota((count, LANES), 1)
    tile_row = jnp.where(
        row < RAD, 16 + TH - RAD + row, jnp.where(row < RAD + TH, row - RAD, 32 + row - RAD - TH)
    )
    pick = jnp.where(lane == tile_row, 1.0, 0.0).astype(BF)
    dead = jnp.dot(pick, dead_tile, preferred_element_type=F32)
    dead_part = jnp.where(lane == tile_col, dead, 0.0)
    row_part = jnp.where(jnp.abs(row - RAD - (lane - 32)) > RAD, 1.0, 0.0)
    col_part = jnp.where(jnp.abs(col - (lane - 40)) > RAD, 1.0, 0.0)
    pad_part = jnp.where((lane == 72) & padded, 1.0, 0.0)
    out = jnp.where(
        lane < 32, dead_part, jnp.where(lane < 40, row_part, jnp.where(lane < 72, col_part, pad_part))
    )
    return (out * FAR).astype(BF)


def kernel(
    groups, nx, ny,
    k_hbm, v_hbm, q_hbm, g_hbm, tissue_ref,
    o_hbm, dq_hbm, dk_hbm, dv_hbm,
    kv, q_buf, g_buf, feat, qfeat, sel, sel_t, dead, dead32, live_q,
    hsend, centre, own, part, hret_out, hret_in, xret_out, xret_in, zret_out, zret_in,
    o_buf, dq_buf, dk_buf, dv_buf,
    side_relay_back,
    in_sem, out_sem, zf_send, zf_recv, xf_send, xf_recv, hf_send, hf_recv, hr_send, hr_recv,
    xr_send, xr_recv, zr_send, zr_recv,
    lv_send, lv_recv, lh_send, lh_recv,
    sb_send, sb_recv,
):
    gx, gy = lax.axis_index("gx"), lax.axis_index("gy")
    has_up, has_down = gy > 0, gy < ny - 1
    has_left, has_right = gx > 0, gx < nx - 1
    up = (gx, jnp.maximum(gy - 1, 0))
    down = (gx, jnp.minimum(gy + 1, ny - 1))
    left = (jnp.maximum(gx - 1, 0), gy)
    right = (jnp.minimum(gx + 1, nx - 1), gy)
    odd = lax.rem(gy, 2)
    even_row = odd == 0
    partner = (gx, gy + 1 - 2 * odd)
    has_next = jnp.where(even_row, gy < ny - 2, gy >= 2)
    has_last = jnp.where(even_row, gy >= 2, gy < ny - 2)
    next_tile = (gx, jnp.clip(gy + 2 - 4 * odd, 0, ny - 1))
    last_tile = (gx, jnp.clip(gy - 2 + 4 * odd, 0, ny - 1))

    half = nx // 2
    seam = (gx == half - 1) | (gx == half)
    at_seam = ((gx == half), (gx == half - 1))
    routes = 3
    by_way = (tuple(2 * n for n in range(routes)), tuple(nx - 1 - 2 * n for n in range(routes)))

    def side_route(g):
        return jnp.where((g >= 1) & (g <= 6), 1 + lax.rem(g - 1, routes), 0)

    def relay_of(g, way):
        number = jnp.maximum(side_route(g) - 1, 0)
        return (2 * number if way == 0 else nx - 1 - 2 * number, gy)

    def side_picked(g):
        return side_route(g) > 0

    def hands_sides(g, way):
        return side_picked(g) & (gx == relay_of(g, way)[0])

    seam_to = ((half - 1, gy), (half, gy))
    on_route = (gx == by_way[0][0])
    for spot in by_way[0][1:] + by_way[1]:
        on_route = on_route | (gx == spot)

    sides = [
        (has_up, up), (has_down, down), (has_left, left), (has_right, right),
        (has_next, next_tile), (has_last, last_tile),
    ]
    sides += [(seam, (spot, gy)) for spot in by_way[0] + by_way[1]]
    sides += [(on_route, spot) for spot in seam_to]

    def lanes_of(g):
        return pl.ds(pl.multiple_of(g * LANES, LANES), LANES)

    def remote(src, dst, send, recv, where):
        return pltpu.make_async_remote_copy(
            src_ref=src, dst_ref=dst, send_sem=send, recv_sem=recv,
            device_id=where, device_id_type=MESH,
        )

    def loads(g):
        at = lanes_of(g)
        mid = pl.ds(OWN, OWN)
        return [
            pltpu.make_async_copy(k_hbm.at[:, at], kv.at[g, mid, pl.ds(0, LANES)], in_sem.at[g, 0]),
            pltpu.make_async_copy(v_hbm.at[:, at], kv.at[g, mid, pl.ds(LANES, LANES)], in_sem.at[g, 1]),
            pltpu.make_async_copy(q_hbm.at[:, at], q_buf.at[g], in_sem.at[g, 2]),
            pltpu.make_async_copy(g_hbm.at[:, at], g_buf.at[g], in_sem.at[g, 3]),
        ]

    def store(g, n):
        buf, hbm = ((o_buf, o_hbm), (dq_buf, dq_hbm), (dk_buf, dk_hbm), (dv_buf, dv_hbm))[n]
        return pltpu.make_async_copy(buf.at[g], hbm.at[:, lanes_of(g)], out_sem.at[g, n])

    def z_forward(g):
        to_rows = pl.ds(pl.multiple_of(odd * (2 * OWN), OWN), OWN)
        return [
            remote(
                hbm.at[:, lanes_of(g)], kv.at[g, to_rows, pl.ds(n * LANES, LANES)],
                zf_send.at[g, n], zf_recv.at[g, n], partner,
            )
            for n, hbm in enumerate((k_hbm, v_hbm))
        ]

    def x_forward(g):
        from_rows = pl.ds(pl.multiple_of((1 - odd) * (SIDES - STRIP), 64), STRIP)
        to_rows = pl.ds(pl.multiple_of(TOP + odd * (STRIP + OWN), 64), STRIP)
        return remote(kv.at[g, from_rows], kv.at[g, to_rows], xf_send.at[g], xf_recv.at[g], next_tile)

    def x_return(g):
        return remote(xret_out.at[g], xret_in.at[g], xr_send.at[g], xr_recv.at[g], last_tile)

    def z_return(g):
        return remote(zret_out.at[g], zret_in.at[g], zr_send.at[g], zr_recv.at[g], partner)

    def h_return_first(g, way):
        return remote(
            hret_out.at[g, pl.ds(way * SLOTS, SLOTS)], side_relay_back.at[g],
            hr_send.at[g, way], sb_recv.at[g], relay_of(g, way),
        )

    def h_return_second(g, way):
        return remote(
            side_relay_back.at[g], hret_in.at[g, pl.ds((1 - way) * SLOTS, SLOTS)],
            sb_send.at[g], hr_recv.at[g, way], seam_to[way],
        )

    def h_forward(g, way):
        to_rows = pl.ds(SIDES + (1 - way) * SLOTS, SLOTS)
        return remote(
            hsend.at[g, pl.ds(way * SLOTS, SLOTS)], kv.at[g, to_rows],
            hf_send.at[g, way], hf_recv.at[g, way], left if way == 0 else right,
        )

    def h_return(g, way):
        return remote(
            hret_out.at[g, pl.ds(way * SLOTS, SLOTS)], hret_in.at[g, pl.ds((1 - way) * SLOTS, SLOTS)],
            hr_send.at[g, way], hr_recv.at[g, way], left if way == 0 else right,
        )

    def live_v(way):
        to_rows = pl.ds(32, 16) if way == 0 else pl.ds(16, 16)
        return remote(
            dead.at[0, pl.ds(0, 16)], dead.at[0, to_rows],
            lv_send.at[way], lv_recv.at[way], up if way == 0 else down,
        )

    def live_h(way):
        return remote(
            dead.at[0, pl.ds(0, 48)], dead.at[2 - way, pl.ds(0, 48)],
            lh_send.at[way], lh_recv.at[way], left if way == 0 else right,
        )

    v_to = (has_up, has_down)
    v_from = (has_down, has_up)
    h_to = (has_left, has_right)
    h_from = (has_right, has_left)

    def send(here, special, direct, first):
        @pl.when(here & jnp.logical_not(special))
        def _():
            for copy in direct():
                copy.start()

        @pl.when(here & special)
        def _():
            for copy in first():
                copy.start()

    def start_rows(g):
        for copy in z_forward(g):
            copy.start()

    dead32[...] = jnp.ones_like(dead32)
    dead32[pl.ds(0, TH), pl.ds(0, TW)] = jnp.where(tissue_ref[...] > 0, 0.0, 1.0)
    dead[...] = jnp.zeros_like(dead)
    dead[0, pl.ds(0, 16), :] = dead32[...].astype(BF)
    for here, tile, first, count in (
        (has_up, 0, 16, 16), (has_down, 0, 32, 16), (has_left, 1, 0, 48), (has_right, 2, 0, 48),
    ):
        @pl.when(jnp.logical_not(here))
        def _():
            dead[tile, pl.ds(first, count), :] = jnp.ones((count, LANES), BF)

    barrier = pltpu.get_barrier_semaphore()
    for here, where in sides:
        @pl.when(here)
        def _():
            pl.semaphore_signal(barrier, inc=1, device_id=where, device_id_type=MESH)
    def start_loads(g, carry):
        for copy in loads(g):
            copy.start()
        return carry

    lax.fori_loop(0, groups, start_loads, 0)

    for here, first, count in (
        (has_up, TOP, STRIP), (has_down, 2 * OWN, STRIP),
        (has_left, SIDES, SLOTS), (has_right, SIDES + SLOTS, SLOTS),
    ):
        @pl.when(jnp.logical_not(here))
        def _():
            def clear(g, carry):
                kv[g, pl.ds(first, count), :] = jnp.zeros((count, 2 * LANES), BF)
                return carry

            lax.fori_loop(0, groups, clear, 0)

    @pl.when(jnp.logical_not(has_next))
    def _():
        def clear(g, carry):
            xret_in[g] = jnp.zeros((STRIP, 2 * LANES), BF)
            return carry

        lax.fori_loop(0, groups, clear, 0)

    for here, first in ((has_left, 0), (has_right, SLOTS)):
        @pl.when(jnp.logical_not(here))
        def _():
            def clear(g, carry):
                hret_in[g, pl.ds(first, SLOTS), :] = jnp.zeros((SLOTS, 2 * LANES), BF)
                return carry

            lax.fori_loop(0, groups, clear, 0)

    peers = sum(here.astype(jnp.int32) for here, _ in sides)
    pl.semaphore_wait(barrier, peers)

    for way in range(2):
        @pl.when(v_to[way])
        def _():
            live_v(way).start()

    def start_forward(g, carry):
        start_rows(g)
        return carry

    lax.fori_loop(0, LEAD, start_forward, 0)

    sel[...] = select_rows((2 * SLOTS, CENTER), 0)
    sel_t[...] = select_rows((CENTER, 2 * SLOTS), 1)
    token, lane = iota((OWN, LANES), 0), iota((OWN, LANES), 1)
    same = (
        (lane < 32)
        | ((lane >= 32) & (lane < 40) & (lane - 32 == token // TW))
        | ((lane >= 40) & (lane < 72) & (lane - 40 == token % TW))
        | (lane == 72)
    )
    qfeat[...] = jnp.where(same, 1.0, 0.0).astype(BF)

    for way in range(2):
        @pl.when(v_from[way])
        def _():
            live_v(way).wait_recv()
    for way in range(2):
        @pl.when(h_to[way])
        def _():
            live_h(way).start()

    tile = dead[0].astype(F32).T.astype(BF)
    row_of, token_of = iota((LANES, OWN), 0), iota((LANES, OWN), 1)
    pick = jnp.where(row_of == token_of // TW, 1.0, 0.0).astype(BF)
    spread = jnp.dot(tile, pick, preferred_element_type=F32)
    dead_q = jnp.sum(jnp.where(row_of == token_of % TW, spread, 0.0), axis=0, keepdims=True)
    live_q[...] = jnp.broadcast_to(1.0 - dead_q, (8, OWN))

    token = iota((CENTER, LANES), 0)
    feat[pl.ds(0, CENTER), :] = key_features(
        token // TW, token % TW, token % TW, token < 0, dead[0]
    )
    for way in range(2):
        @pl.when(h_from[way])
        def _():
            live_h(way).wait_recv()
    slot = iota((SLOTS, LANES), 0)
    row = slot_row(slot)
    col = slot - row * RAD
    none = slot >= SPAN * RAD
    feat[pl.ds(CENTER, SLOTS), :] = key_features(row, col - RAD, col + TW - RAD, none, dead[1])
    feat[pl.ds(CENTER + SLOTS, SLOTS), :] = key_features(row, col + TW, col, none, dead[2])

    def send_sides(g):
        for copy in loads(g):
            copy.wait()

        @pl.when(has_last)
        def _():
            x_forward(g).wait_recv()

        picked = jnp.dot(sel[...], kv[g, pl.ds(TOP, CENTER), :], preferred_element_type=F32)
        hsend[g] = picked.astype(BF)
        for way in range(2):
            @pl.when(h_to[way])
            def _():
                h_forward(g, way).start()

    def attend(g):
        for way in range(2):
            @pl.when(h_from[way])
            def _():
                h_forward(g, way).wait_recv()
        contract = (((1,), (1,)), ((), ()))
        query = q_buf[g] * (HD ** -0.5)
        grad = g_buf[g]
        head_of = iota((OWN, LANES), 1) // HD
        nothing = jnp.zeros((OWN, LANES), BF)
        queries_h = [jnp.where(head_of == head, query, nothing) for head in range(2)]
        grads_h = [jnp.where(head_of == head, grad, nothing) for head in range(2)]
        grad_t = grad.T.astype(F32)
        side_keys, side_values = (kv[g, pl.ds(SIDES, 2 * SLOTS), pl.ds(n, LANES)] for n in (0, LANES))
        mid_keys, mid_values = (kv[g, pl.ds(TOP, CENTER), pl.ds(n, LANES)] for n in (0, LANES))
        side_keys_t, side_values_t = side_keys.T, side_values.T
        mid_keys_t, mid_values_t = mid_keys.T, mid_values.T

        def tokens_of(half):
            return slice(half * HALF, (half + 1) * HALF)

        def reach_of(half):
            return slice(half * HALF, half * HALF + REACH)

        def both(pair, half):
            return jnp.concatenate([x[tokens_of(half)] for x in pair], axis=0)

        def keys_of(half, mid, side):
            return jnp.concatenate([mid[reach_of(half)], side], axis=0)

        def keys_t_of(half, mid, side):
            return jnp.concatenate([mid[:, reach_of(half)], side], axis=1)

        def scores_of(half):
            feats = keys_of(half, feat[pl.ds(0, CENTER), :], feat[pl.ds(CENTER, 2 * SLOTS), :])
            own_feats = qfeat[pl.ds(half * HALF, HALF), :]
            return lax.dot_general(
                jnp.concatenate([keys_of(half, mid_keys, side_keys), feats], axis=1),
                jnp.concatenate(
                    [both(queries_h, half), jnp.concatenate([own_feats, own_feats], axis=0)], axis=1
                ),
                contract, preferred_element_type=F32,
            )

        def attention_of(half, scores):
            live = live_q[pl.ds(0, 1), pl.ds(half * HALF, HALF)]
            top = jnp.max(scores, axis=0, keepdims=True)
            raised = jnp.exp(scores - top)
            total = jnp.sum(raised, axis=0, keepdims=True)
            return raised * (jnp.concatenate([live, live], axis=1) / total)

        def per_head(out):
            return jnp.concatenate([out[:HD, :HALF], out[HD:, HALF:]], axis=0)

        def attended_of(half, weight):
            out = jnp.dot(
                keys_t_of(half, mid_values_t, side_values_t), weight, preferred_element_type=F32
            )
            return per_head(out).astype(BF).astype(F32)

        def delta_of(half, out):
            terms = out * grad_t[:, tokens_of(half)]
            return jnp.concatenate(
                [jnp.sum(terms[:HD], axis=0, keepdims=True), jnp.sum(terms[HD:], axis=0, keepdims=True)], axis=1
            )

        def grad_prob_of(half):
            return lax.dot_general(
                keys_of(half, mid_values, side_values), both(grads_h, half), contract,
                preferred_element_type=F32,
            )

        def query_grad_of(half, grad_score):
            return per_head(
                jnp.dot(keys_t_of(half, mid_keys_t, side_keys_t), grad_score, preferred_element_type=F32)
            )

        scores_0, scores_1 = scores_of(0), scores_of(1)
        attention_0 = attention_of(0, scores_0)
        weight_0 = attention_0.astype(BF)
        prob_0 = grad_prob_of(0)
        out_0 = attended_of(0, weight_0)
        attention_1 = attention_of(1, scores_1)
        weight_1 = attention_1.astype(BF)
        prob_1 = grad_prob_of(1)
        delta_0 = delta_of(0, out_0)
        out_1 = attended_of(1, weight_1)
        score_0 = (attention_0 * (prob_0 - delta_0)).astype(BF)
        delta_1 = delta_of(1, out_1)
        query_grad_0 = query_grad_of(0, score_0)
        score_1 = (attention_1 * (prob_1 - delta_1)).astype(BF)
        query_grad_1 = query_grad_of(1, score_1)

        def key_sums(factors, rows_h):
            first, second = (
                jnp.dot(factor, both(rows_h, half), preferred_element_type=F32)
                for half, factor in enumerate(factors)
            )
            middle = first[HALF:REACH] + second[: REACH - HALF]
            mid = jnp.concatenate([first[:HALF], middle, second[REACH - HALF : REACH]], axis=0)
            return mid, first[REACH:] + second[REACH:]

        key_mid, key_side = key_sums((score_0, score_1), queries_h)
        value_mid, value_side = key_sums((weight_0, weight_1), grads_h)
        o_buf[g] = jnp.concatenate([out_0, out_1], axis=1).T.astype(BF)
        dq_buf[g] = (jnp.concatenate([query_grad_0, query_grad_1], axis=1) * (HD ** -0.5)).T.astype(BF)
        store(g, 0).start()
        store(g, 1).start()
        centre[lax.rem(g, 3)] = jnp.concatenate([key_mid, value_mid], axis=1)
        hret_out[g] = jnp.concatenate([key_side, value_side], axis=1).astype(BF)
        for way in range(2):
            send(
                h_to[way], at_seam[way] & side_picked(g),
                lambda: [h_return(g, way)], lambda: [h_return_first(g, way)],
            )

    def send_rows(g):
        for way in range(2):
            @pl.when(h_from[way])
            def _():
                h_return(g, way).wait_recv()
        sums = centre[lax.rem(g, 3)] + jnp.dot(sel_t[...], hret_in[g], preferred_element_type=F32)
        own[g] = sums[STRIP : STRIP + OWN]
        above, below = sums[:STRIP], sums[STRIP + OWN :]

        @pl.when(even_row)
        def _():
            xret_out[g] = above.astype(BF)
            part[g] = below

        @pl.when(jnp.logical_not(even_row))
        def _():
            xret_out[g] = below.astype(BF)
            part[g] = above

        @pl.when(has_last)
        def _():
            x_return(g).start()

    def send_partner(g):
        @pl.when(has_next)
        def _():
            x_return(g).wait_recv()

        mine, other = part[g], xret_in[g].astype(F32)
        first, second = jnp.where(even_row, mine, other), jnp.where(even_row, other, mine)
        cut, tail = OWN - STRIP, 2 * STRIP - OWN
        zret_out[g] = jnp.concatenate(
            [first[:cut], first[cut:] + second[:tail], second[tail:]], axis=0
        ).astype(BF)
        z_return(g).start()

    def hand_rows(g):
        for copy in z_forward(g):
            copy.wait_recv()

        @pl.when(has_next)
        def _():
            x_forward(g).start()

    def hand_sides_back(g):
        for way in range(2):
            @pl.when(hands_sides(g, way))
            def _():
                h_return_first(g, way).wait_recv()
                h_return_second(g, way).start()

    def step(i, carry):
        def stage(lag, work):
            @pl.when((i >= lag) & (i < groups + lag))
            def _():
                work(i - lag)

        for n in range(RATE):
            @pl.when(LEAD + RATE * i + n < groups)
            def _():
                start_rows(LEAD + RATE * i + n)

        stage(-1, hand_rows)
        stage(0, send_sides)
        stage(2, attend)
        stage(3, hand_sides_back)
        stage(4, send_rows)
        stage(5, send_partner)
        return carry

    hand_rows(0)
    lax.fori_loop(0, groups + 5, step, 0)

    def drain(g, carry):
        store(g, 0).wait()
        store(g, 1).wait()
        for copy in z_forward(g):
            copy.wait_send()

        @pl.when(has_next)
        def _():
            x_forward(g).wait_send()

        @pl.when(has_last)
        def _():
            x_return(g).wait_send()

        for way in range(2):
            @pl.when(h_to[way])
            def _():
                h_forward(g, way).wait_send()
                h_return(g, way).wait_send()

        @pl.when(hands_sides(g, 0) | hands_sides(g, 1))
        def _():
            h_return_second(g, 0).wait_send()

        return carry

    lax.fori_loop(0, groups, drain, 0)
    for way in range(2):
        @pl.when(v_to[way])
        def _():
            live_v(way).wait_send()

        @pl.when(h_to[way])
        def _():
            live_h(way).wait_send()

    def finish(g, carry):
        z_return(g).wait_recv()
        total = own[g] + zret_in[g].astype(F32)
        dk_buf[g] = total[:, :LANES].astype(BF)
        dv_buf[g] = total[:, LANES:].astype(BF)
        store(g, 2).start()
        store(g, 3).start()
        return carry

    lax.fori_loop(0, groups, finish, 0)

    def drain_last(g, carry):
        z_return(g).wait_send()
        store(g, 2).wait()
        store(g, 3).wait()
        return carry

    lax.fori_loop(0, groups, drain_last, 0)


def write_out(*refs):
    ins, outs, bufs, sem = refs[:4], refs[4:8], refs[8:12], refs[12]
    reads = [pltpu.make_async_copy(a, b, sem.at[0, n]) for n, (a, b) in enumerate(zip(ins, bufs))]
    writes = [pltpu.make_async_copy(a, b, sem.at[1, n]) for n, (a, b) in enumerate(zip(bufs, outs))]
    for copy in reads:
        copy.start()
    for read, write in zip(reads, writes):
        read.wait()
        write.start()
    for copy in writes:
        copy.wait()


def per_device(queries, keys, values, out_grad, tissue):
    width = queries.shape[-1]
    groups = width // LANES
    flat = (OWN, width)
    any_spec = pl.BlockSpec(memory_space=pl.ANY)
    dma = pltpu.SemaphoreType.DMA
    outs = pl.pallas_call(
        functools.partial(kernel, groups, lax.axis_size("gx"), lax.axis_size("gy")),
        out_shape=[jax.ShapeDtypeStruct(flat, BF)] * 4,
        in_specs=[any_spec] * 4 + [pl.BlockSpec(memory_space=pltpu.VMEM)],
        out_specs=[any_spec] * 4,
        scratch_shapes=[
            pltpu.VMEM((groups, ROWS, 2 * LANES), BF),
            pltpu.VMEM((groups, OWN, LANES), BF),
            pltpu.VMEM((groups, OWN, LANES), BF),
            pltpu.VMEM((KEYS, LANES), BF),
            pltpu.VMEM((OWN, LANES), BF),
            pltpu.VMEM((2 * SLOTS, CENTER), BF),
            pltpu.VMEM((CENTER, 2 * SLOTS), BF),
            pltpu.VMEM((3, LANES, LANES), BF),
            pltpu.VMEM((16, LANES), F32),
            pltpu.VMEM((8, OWN), F32),
            pltpu.VMEM((groups, 2 * SLOTS, 2 * LANES), BF),
            pltpu.VMEM((3, CENTER, 2 * LANES), F32),
            pltpu.VMEM((groups, OWN, 2 * LANES), F32),
            pltpu.VMEM((groups, STRIP, 2 * LANES), F32),
            pltpu.VMEM((groups, 2 * SLOTS, 2 * LANES), BF),
            pltpu.VMEM((groups, 2 * SLOTS, 2 * LANES), BF),
            pltpu.VMEM((groups, STRIP, 2 * LANES), BF),
            pltpu.VMEM((groups, STRIP, 2 * LANES), BF),
            pltpu.VMEM((groups, OWN, 2 * LANES), BF),
            pltpu.VMEM((groups, OWN, 2 * LANES), BF),
            pltpu.VMEM((groups, OWN, LANES), BF),
            pltpu.VMEM((groups, OWN, LANES), BF),
            pltpu.VMEM((groups, OWN, LANES), BF),
            pltpu.VMEM((groups, OWN, LANES), BF),
            pltpu.VMEM((groups, SLOTS, 2 * LANES), BF),
            dma((groups, 4)), dma((groups, 4)),
            dma((groups, 2)), dma((groups, 2)), dma((groups,)), dma((groups,)),
            dma((groups, 2)), dma((groups, 2)), dma((groups, 2)), dma((groups, 2)),
            dma((groups,)), dma((groups,)), dma((groups,)), dma((groups,)),
            dma((2,)), dma((2,)), dma((2,)), dma((2,)),
            dma((groups,)), dma((groups,)),
        ],
        compiler_params=pltpu.CompilerParams(
            collective_id=0, has_side_effects=True, vmem_limit_bytes=56 * 1024 * 1024
        ),
    )(
        keys.reshape(flat), values.reshape(flat), queries.reshape(flat), out_grad.reshape(flat),
        tissue,
    )
    outs = pl.pallas_call(
        write_out,
        out_shape=[jax.ShapeDtypeStruct(flat, BF)] * 4,
        in_specs=[any_spec] * 4,
        out_specs=[any_spec] * 4,
        scratch_shapes=[pltpu.VMEM(flat, BF)] * 4 + [dma((2, 4))],
    )(*outs)
    return tuple(out.reshape(queries.shape) for out in outs)


def solution(mesh):
    tokens = P("gy", "gx", None)
    return jax.shard_map(
        per_device, mesh=mesh, in_specs=(tokens,) * 4 + (P("gy", "gx"),),
        out_specs=(tokens,) * 4, check_vma=False,
    )
```

```python
import functools

import jax
import jax.numpy as jnp
from jax import lax
from jax.experimental import pallas as pl
from jax.experimental.pallas import tpu as pltpu
from jax.sharding import PartitionSpec as P

MESH = pl.DeviceIdType.MESH
HD = 64
RAD = 6
TH = 8
TW = 32
LANES = 128
OWN = TH * TW
STRIP = RAD * TW
CENTER = OWN + 2 * STRIP
SPAN = TH + 2 * RAD
SLOTS = 128
KEYS = CENTER + 2 * SLOTS
TOP = OWN - STRIP
SIDES = 3 * OWN
ROWS = SIDES + 2 * SLOTS
HALF = OWN // 2
REACH = HALF + 2 * STRIP
FAR = -1e30
LEAD = 3
RATE = 1
BF = jnp.bfloat16
F32 = jnp.float32


def iota(shape, dim):
    return lax.broadcasted_iota(jnp.int32, shape, dim)


def slot_row(slot):
    return jnp.floor((slot.astype(F32) + 0.5) * (1.0 / RAD)).astype(jnp.int32)


def select_rows(shape, slot_dim):
    slot_all, token = iota(shape, slot_dim), iota(shape, 1 - slot_dim)
    right = slot_all >= SLOTS
    slot = jnp.where(right, slot_all - SLOTS, slot_all)
    row = slot_row(slot)
    col = slot - row * RAD + jnp.where(right, TW - RAD, 0)
    hit = (slot < SPAN * RAD) & (token == row * TW + col)
    return jnp.where(hit, 1.0, 0.0).astype(BF)


def key_features(row, col, tile_col, padded, dead_tile):
    count = row.shape[0]
    lane = iota((count, LANES), 1)
    tile_row = jnp.where(
        row < RAD, 16 + TH - RAD + row, jnp.where(row < RAD + TH, row - RAD, 32 + row - RAD - TH)
    )
    pick = jnp.where(lane == tile_row, 1.0, 0.0).astype(BF)
    dead = jnp.dot(pick, dead_tile, preferred_element_type=F32)
    dead_part = jnp.where(lane == tile_col, dead, 0.0)
    row_part = jnp.where(jnp.abs(row - RAD - (lane - 32)) > RAD, 1.0, 0.0)
    col_part = jnp.where(jnp.abs(col - (lane - 40)) > RAD, 1.0, 0.0)
    pad_part = jnp.where((lane == 72) & padded, 1.0, 0.0)
    out = jnp.where(
        lane < 32, dead_part, jnp.where(lane < 40, row_part, jnp.where(lane < 72, col_part, pad_part))
    )
    return (out * FAR).astype(BF)


def kernel(
    groups, nx, ny,
    k_hbm, v_hbm, q_hbm, g_hbm, tissue_ref,
    o_hbm, dq_hbm, dk_hbm, dv_hbm,
    kv, q_buf, g_buf, feat, qfeat, sel, sel_t, dead, dead32, live_q,
    hsend, centre, own, part, hret_out, hret_in, xret_out, xret_in, zret_out, zret_in,
    o_buf, dq_buf, dk_buf, dv_buf,
    side_relay_back,
    in_sem, out_sem, zf_send, zf_recv, xf_send, xf_recv, hf_send, hf_recv, hr_send, hr_recv,
    xr_send, xr_recv, zr_send, zr_recv,
    lv_send, lv_recv, lh_send, lh_recv,
    sb_send, sb_recv,
):
    gx, gy = lax.axis_index("gx"), lax.axis_index("gy")
    has_up, has_down = gy > 0, gy < ny - 1
    has_left, has_right = gx > 0, gx < nx - 1
    up = (gx, jnp.maximum(gy - 1, 0))
    down = (gx, jnp.minimum(gy + 1, ny - 1))
    left = (jnp.maximum(gx - 1, 0), gy)
    right = (jnp.minimum(gx + 1, nx - 1), gy)
    odd = lax.rem(gy, 2)
    even_row = odd == 0
    partner = (gx, gy + 1 - 2 * odd)
    has_next = jnp.where(even_row, gy < ny - 2, gy >= 2)
    has_last = jnp.where(even_row, gy >= 2, gy < ny - 2)
    next_tile = (gx, jnp.clip(gy + 2 - 4 * odd, 0, ny - 1))
    last_tile = (gx, jnp.clip(gy - 2 + 4 * odd, 0, ny - 1))

    half = nx // 2
    seam = (gx == half - 1) | (gx == half)
    at_seam = ((gx == half), (gx == half - 1))
    routes = 3
    by_way = (tuple(2 * n for n in range(routes)), tuple(nx - 1 - 2 * n for n in range(routes)))

    def side_route(g):
        return jnp.where((g >= 1) & (g <= 6), 1 + lax.rem(g - 1, routes), 0)

    def relay_of(g, way):
        number = jnp.maximum(side_route(g) - 1, 0)
        return (2 * number if way == 0 else nx - 1 - 2 * number, gy)

    def side_picked(g):
        return side_route(g) > 0

    def hands_sides(g, way):
        return side_picked(g) & (gx == relay_of(g, way)[0])

    seam_to = ((half - 1, gy), (half, gy))
    on_route = (gx == by_way[0][0])
    for spot in by_way[0][1:] + by_way[1]:
        on_route = on_route | (gx == spot)

    sides = [
        (has_up, up), (has_down, down), (has_left, left), (has_right, right),
        (has_next, next_tile), (has_last, last_tile),
    ]
    sides += [(seam, (spot, gy)) for spot in by_way[0] + by_way[1]]
    sides += [(on_route, spot) for spot in seam_to]

    def lanes_of(g):
        return pl.ds(pl.multiple_of(g * LANES, LANES), LANES)

    def remote(src, dst, send, recv, where):
        return pltpu.make_async_remote_copy(
            src_ref=src, dst_ref=dst, send_sem=send, recv_sem=recv,
            device_id=where, device_id_type=MESH,
        )

    def loads(g):
        at = lanes_of(g)
        mid = pl.ds(OWN, OWN)
        return [
            pltpu.make_async_copy(k_hbm.at[:, at], kv.at[g, mid, pl.ds(0, LANES)], in_sem.at[g, 0]),
            pltpu.make_async_copy(v_hbm.at[:, at], kv.at[g, mid, pl.ds(LANES, LANES)], in_sem.at[g, 1]),
            pltpu.make_async_copy(q_hbm.at[:, at], q_buf.at[g], in_sem.at[g, 2]),
            pltpu.make_async_copy(g_hbm.at[:, at], g_buf.at[g], in_sem.at[g, 3]),
        ]

    def store(g, n):
        buf, hbm = ((o_buf, o_hbm), (dq_buf, dq_hbm), (dk_buf, dk_hbm), (dv_buf, dv_hbm))[n]
        return pltpu.make_async_copy(buf.at[g], hbm.at[:, lanes_of(g)], out_sem.at[g, n])

    def z_forward(g):
        to_rows = pl.ds(pl.multiple_of(odd * (2 * OWN), OWN), OWN)
        return [
            remote(
                hbm.at[:, lanes_of(g)], kv.at[g, to_rows, pl.ds(n * LANES, LANES)],
                zf_send.at[g, n], zf_recv.at[g, n], partner,
            )
            for n, hbm in enumerate((k_hbm, v_hbm))
        ]

    def x_forward(g):
        from_rows = pl.ds(pl.multiple_of((1 - odd) * (SIDES - STRIP), 64), STRIP)
        to_rows = pl.ds(pl.multiple_of(TOP + odd * (STRIP + OWN), 64), STRIP)
        return remote(kv.at[g, from_rows], kv.at[g, to_rows], xf_send.at[g], xf_recv.at[g], next_tile)

    def x_return(g):
        return remote(xret_out.at[g], xret_in.at[g], xr_send.at[g], xr_recv.at[g], last_tile)

    def z_return(g):
        return remote(zret_out.at[g], zret_in.at[g], zr_send.at[g], zr_recv.at[g], partner)

    def h_return_first(g, way):
        return remote(
            hret_out.at[g, pl.ds(way * SLOTS, SLOTS)], side_relay_back.at[g],
            hr_send.at[g, way], sb_recv.at[g], relay_of(g, way),
        )

    def h_return_second(g, way):
        return remote(
            side_relay_back.at[g], hret_in.at[g, pl.ds((1 - way) * SLOTS, SLOTS)],
            sb_send.at[g], hr_recv.at[g, way], seam_to[way],
        )

    def h_forward(g, way):
        to_rows = pl.ds(SIDES + (1 - way) * SLOTS, SLOTS)
        return remote(
            hsend.at[g, pl.ds(way * SLOTS, SLOTS)], kv.at[g, to_rows],
            hf_send.at[g, way], hf_recv.at[g, way], left if way == 0 else right,
        )

    def h_return(g, way):
        return remote(
            hret_out.at[g, pl.ds(way * SLOTS, SLOTS)], hret_in.at[g, pl.ds((1 - way) * SLOTS, SLOTS)],
            hr_send.at[g, way], hr_recv.at[g, way], left if way == 0 else right,
        )

    def live_v(way):
        to_rows = pl.ds(32, 16) if way == 0 else pl.ds(16, 16)
        return remote(
            dead.at[0, pl.ds(0, 16)], dead.at[0, to_rows],
            lv_send.at[way], lv_recv.at[way], up if way == 0 else down,
        )

    def live_h(way):
        return remote(
            dead.at[0, pl.ds(0, 48)], dead.at[2 - way, pl.ds(0, 48)],
            lh_send.at[way], lh_recv.at[way], left if way == 0 else right,
        )

    v_to = (has_up, has_down)
    v_from = (has_down, has_up)
    h_to = (has_left, has_right)
    h_from = (has_right, has_left)

    def send(here, special, direct, first):
        @pl.when(here & jnp.logical_not(special))
        def _():
            for copy in direct():
                copy.start()

        @pl.when(here & special)
        def _():
            for copy in first():
                copy.start()

    def start_rows(g):
        for copy in z_forward(g):
            copy.start()

    dead32[...] = jnp.ones_like(dead32)
    dead32[pl.ds(0, TH), pl.ds(0, TW)] = jnp.where(tissue_ref[...] > 0, 0.0, 1.0)
    dead[...] = jnp.zeros_like(dead)
    dead[0, pl.ds(0, 16), :] = dead32[...].astype(BF)
    for here, tile, first, count in (
        (has_up, 0, 16, 16), (has_down, 0, 32, 16), (has_left, 1, 0, 48), (has_right, 2, 0, 48),
    ):
        @pl.when(jnp.logical_not(here))
        def _():
            dead[tile, pl.ds(first, count), :] = jnp.ones((count, LANES), BF)

    barrier = pltpu.get_barrier_semaphore()
    for here, where in sides:
        @pl.when(here)
        def _():
            pl.semaphore_signal(barrier, inc=1, device_id=where, device_id_type=MESH)
    def start_loads(g, carry):
        for copy in loads(g):
            copy.start()
        return carry

    lax.fori_loop(0, groups, start_loads, 0)

    for here, first, count in (
        (has_up, TOP, STRIP), (has_down, 2 * OWN, STRIP),
        (has_left, SIDES, SLOTS), (has_right, SIDES + SLOTS, SLOTS),
    ):
        @pl.when(jnp.logical_not(here))
        def _():
            def clear(g, carry):
                kv[g, pl.ds(first, count), :] = jnp.zeros((count, 2 * LANES), BF)
                return carry

            lax.fori_loop(0, groups, clear, 0)

    @pl.when(jnp.logical_not(has_next))
    def _():
        def clear(g, carry):
            xret_in[g] = jnp.zeros((STRIP, 2 * LANES), BF)
            return carry

        lax.fori_loop(0, groups, clear, 0)

    for here, first in ((has_left, 0), (has_right, SLOTS)):
        @pl.when(jnp.logical_not(here))
        def _():
            def clear(g, carry):
                hret_in[g, pl.ds(first, SLOTS), :] = jnp.zeros((SLOTS, 2 * LANES), BF)
                return carry

            lax.fori_loop(0, groups, clear, 0)

    peers = sum(here.astype(jnp.int32) for here, _ in sides)
    pl.semaphore_wait(barrier, peers)

    for way in range(2):
        @pl.when(v_to[way])
        def _():
            live_v(way).start()

    def start_forward(g, carry):
        start_rows(g)
        return carry

    lax.fori_loop(0, LEAD, start_forward, 0)

    sel[...] = select_rows((2 * SLOTS, CENTER), 0)
    sel_t[...] = select_rows((CENTER, 2 * SLOTS), 1)
    token, lane = iota((OWN, LANES), 0), iota((OWN, LANES), 1)
    same = (
        (lane < 32)
        | ((lane >= 32) & (lane < 40) & (lane - 32 == token // TW))
        | ((lane >= 40) & (lane < 72) & (lane - 40 == token % TW))
        | (lane == 72)
    )
    qfeat[...] = jnp.where(same, 1.0, 0.0).astype(BF)

    for way in range(2):
        @pl.when(v_from[way])
        def _():
            live_v(way).wait_recv()
    for way in range(2):
        @pl.when(h_to[way])
        def _():
            live_h(way).start()

    tile = dead[0].astype(F32).T.astype(BF)
    row_of, token_of = iota((LANES, OWN), 0), iota((LANES, OWN), 1)
    pick = jnp.where(row_of == token_of // TW, 1.0, 0.0).astype(BF)
    spread = jnp.dot(tile, pick, preferred_element_type=F32)
    dead_q = jnp.sum(jnp.where(row_of == token_of % TW, spread, 0.0), axis=0, keepdims=True)
    live_q[...] = jnp.broadcast_to(1.0 - dead_q, (8, OWN))

    token = iota((CENTER, LANES), 0)
    feat[pl.ds(0, CENTER), :] = key_features(
        token // TW, token % TW, token % TW, token < 0, dead[0]
    )
    for way in range(2):
        @pl.when(h_from[way])
        def _():
            live_h(way).wait_recv()
    slot = iota((SLOTS, LANES), 0)
    row = slot_row(slot)
    col = slot - row * RAD
    none = slot >= SPAN * RAD
    feat[pl.ds(CENTER, SLOTS), :] = key_features(row, col - RAD, col + TW - RAD, none, dead[1])
    feat[pl.ds(CENTER + SLOTS, SLOTS), :] = key_features(row, col + TW, col, none, dead[2])

    def send_sides(g):
        for copy in loads(g):
            copy.wait()

        @pl.when(has_last)
        def _():
            x_forward(g).wait_recv()

        picked = jnp.dot(sel[...], kv[g, pl.ds(TOP, CENTER), :], preferred_element_type=F32)
        hsend[g] = picked.astype(BF)
        for way in range(2):
            @pl.when(h_to[way])
            def _():
                h_forward(g, way).start()

    def attend(g):
        for way in range(2):
            @pl.when(h_from[way])
            def _():
                h_forward(g, way).wait_recv()
        contract = (((1,), (1,)), ((), ()))
        query = q_buf[g] * (HD ** -0.5)
        grad = g_buf[g]
        head_of = iota((OWN, LANES), 1) // HD
        nothing = jnp.zeros((OWN, LANES), BF)
        queries_h = [jnp.where(head_of == head, query, nothing) for head in range(2)]
        grads_h = [jnp.where(head_of == head, grad, nothing) for head in range(2)]
        grad_t = grad.T.astype(F32)
        side_keys, side_values = (kv[g, pl.ds(SIDES, 2 * SLOTS), pl.ds(n, LANES)] for n in (0, LANES))
        mid_keys, mid_values = (kv[g, pl.ds(TOP, CENTER), pl.ds(n, LANES)] for n in (0, LANES))
        side_keys_t, side_values_t = side_keys.T, side_values.T
        mid_keys_t, mid_values_t = mid_keys.T, mid_values.T

        def tokens_of(half):
            return slice(half * HALF, (half + 1) * HALF)

        def reach_of(half):
            return slice(half * HALF, half * HALF + REACH)

        def both(pair, half):
            return jnp.concatenate([x[tokens_of(half)] for x in pair], axis=0)

        def keys_of(half, mid, side):
            return jnp.concatenate([mid[reach_of(half)], side], axis=0)

        def keys_t_of(half, mid, side):
            return jnp.concatenate([mid[:, reach_of(half)], side], axis=1)

        def scores_of(half):
            feats = keys_of(half, feat[pl.ds(0, CENTER), :], feat[pl.ds(CENTER, 2 * SLOTS), :])
            own_feats = qfeat[pl.ds(half * HALF, HALF), :]
            return lax.dot_general(
                jnp.concatenate([keys_of(half, mid_keys, side_keys), feats], axis=1),
                jnp.concatenate(
                    [both(queries_h, half), jnp.concatenate([own_feats, own_feats], axis=0)], axis=1
                ),
                contract, preferred_element_type=F32,
            )

        def attention_of(half, scores):
            live = live_q[pl.ds(0, 1), pl.ds(half * HALF, HALF)]
            top = jnp.max(scores, axis=0, keepdims=True)
            raised = jnp.exp(scores - top)
            total = jnp.sum(raised, axis=0, keepdims=True)
            return raised * (jnp.concatenate([live, live], axis=1) / total)

        def per_head(out):
            return jnp.concatenate([out[:HD, :HALF], out[HD:, HALF:]], axis=0)

        def attended_of(half, weight):
            out = jnp.dot(
                keys_t_of(half, mid_values_t, side_values_t), weight, preferred_element_type=F32
            )
            return per_head(out).astype(BF).astype(F32)

        def delta_of(half, out):
            terms = out * grad_t[:, tokens_of(half)]
            return jnp.concatenate(
                [jnp.sum(terms[:HD], axis=0, keepdims=True), jnp.sum(terms[HD:], axis=0, keepdims=True)], axis=1
            )

        def grad_prob_of(half):
            return lax.dot_general(
                keys_of(half, mid_values, side_values), both(grads_h, half), contract,
                preferred_element_type=F32,
            )

        def query_grad_of(half, grad_score):
            return per_head(
                jnp.dot(keys_t_of(half, mid_keys_t, side_keys_t), grad_score, preferred_element_type=F32)
            )

        scores_0, scores_1 = scores_of(0), scores_of(1)
        attention_0 = attention_of(0, scores_0)
        weight_0 = attention_0.astype(BF)
        prob_0 = grad_prob_of(0)
        out_0 = attended_of(0, weight_0)
        attention_1 = attention_of(1, scores_1)
        weight_1 = attention_1.astype(BF)
        prob_1 = grad_prob_of(1)
        delta_0 = delta_of(0, out_0)
        out_1 = attended_of(1, weight_1)
        score_0 = (attention_0 * (prob_0 - delta_0)).astype(BF)
        delta_1 = delta_of(1, out_1)
        query_grad_0 = query_grad_of(0, score_0)
        score_1 = (attention_1 * (prob_1 - delta_1)).astype(BF)
        query_grad_1 = query_grad_of(1, score_1)

        def key_sums(factors, rows_h):
            first, second = (
                jnp.dot(factor, both(rows_h, half), preferred_element_type=F32)
                for half, factor in enumerate(factors)
            )
            middle = first[HALF:REACH] + second[: REACH - HALF]
            mid = jnp.concatenate([first[:HALF], middle, second[REACH - HALF : REACH]], axis=0)
            return mid, first[REACH:] + second[REACH:]

        key_mid, key_side = key_sums((score_0, score_1), queries_h)
        value_mid, value_side = key_sums((weight_0, weight_1), grads_h)
        o_buf[g] = jnp.concatenate([out_0, out_1], axis=1).T.astype(BF)
        dq_buf[g] = (jnp.concatenate([query_grad_0, query_grad_1], axis=1) * (HD ** -0.5)).T.astype(BF)
        store(g, 0).start()
        store(g, 1).start()
        centre[lax.rem(g, 3)] = jnp.concatenate([key_mid, value_mid], axis=1)
        hret_out[g] = jnp.concatenate([key_side, value_side], axis=1).astype(BF)
        for way in range(2):
            send(
                h_to[way], at_seam[way] & side_picked(g),
                lambda: [h_return(g, way)], lambda: [h_return_first(g, way)],
            )

    def send_rows(g):
        for way in range(2):
            @pl.when(h_from[way])
            def _():
                h_return(g, way).wait_recv()
        sums = centre[lax.rem(g, 3)] + jnp.dot(sel_t[...], hret_in[g], preferred_element_type=F32)
        own[g] = sums[STRIP : STRIP + OWN]
        above, below = sums[:STRIP], sums[STRIP + OWN :]

        @pl.when(even_row)
        def _():
            xret_out[g] = above.astype(BF)
            part[g] = below

        @pl.when(jnp.logical_not(even_row))
        def _():
            xret_out[g] = below.astype(BF)
            part[g] = above

        @pl.when(has_last)
        def _():
            x_return(g).start()

    def send_partner(g):
        @pl.when(has_next)
        def _():
            x_return(g).wait_recv()

        mine, other = part[g], xret_in[g].astype(F32)
        first, second = jnp.where(even_row, mine, other), jnp.where(even_row, other, mine)
        cut, tail = OWN - STRIP, 2 * STRIP - OWN
        zret_out[g] = jnp.concatenate(
            [first[:cut], first[cut:] + second[:tail], second[tail:]], axis=0
        ).astype(BF)
        z_return(g).start()

    def hand_rows(g):
        for copy in z_forward(g):
            copy.wait_recv()

        @pl.when(has_next)
        def _():
            x_forward(g).start()

    def hand_sides_back(g):
        for way in range(2):
            @pl.when(hands_sides(g, way))
            def _():
                h_return_first(g, way).wait_recv()
                h_return_second(g, way).start()

    def step(i, carry):
        def stage(lag, work):
            @pl.when((i >= lag) & (i < groups + lag))
            def _():
                work(i - lag)

        for n in range(RATE):
            @pl.when(LEAD + RATE * i + n < groups)
            def _():
                start_rows(LEAD + RATE * i + n)

        stage(-1, hand_rows)
        stage(0, send_sides)
        stage(2, attend)
        stage(3, hand_sides_back)
        stage(4, send_rows)
        stage(5, send_partner)
        return carry

    hand_rows(0)
    lax.fori_loop(0, groups + 5, step, 0)

    def drain(g, carry):
        store(g, 0).wait()
        store(g, 1).wait()
        for copy in z_forward(g):
            copy.wait_send()

        @pl.when(has_next)
        def _():
            x_forward(g).wait_send()

        @pl.when(has_last)
        def _():
            x_return(g).wait_send()

        for way in range(2):
            @pl.when(h_to[way])
            def _():
                h_forward(g, way).wait_send()
                h_return(g, way).wait_send()

        @pl.when(hands_sides(g, 0) | hands_sides(g, 1))
        def _():
            h_return_second(g, 0).wait_send()

        return carry

    lax.fori_loop(0, groups, drain, 0)
    for way in range(2):
        @pl.when(v_to[way])
        def _():
            live_v(way).wait_send()

        @pl.when(h_to[way])
        def _():
            live_h(way).wait_send()

    def finish(g, carry):
        z_return(g).wait_recv()
        total = own[g] + zret_in[g].astype(F32)
        dk_buf[g] = total[:, :LANES].astype(BF)
        dv_buf[g] = total[:, LANES:].astype(BF)
        store(g, 2).start()
        store(g, 3).start()
        return carry

    lax.fori_loop(0, groups, finish, 0)

    def drain_last(g, carry):
        z_return(g).wait_send()
        store(g, 2).wait()
        store(g, 3).wait()
        return carry

    lax.fori_loop(0, groups, drain_last, 0)


def write_out(*refs):
    ins, outs, bufs, sem = refs[:4], refs[4:8], refs[8:12], refs[12]
    cuts = [(n, c, pl.ds(c * (OWN // 4), OWN // 4)) for c in range(4) for n in range(4)]
    reads = [pltpu.make_async_copy(ins[n].at[at], bufs[n].at[at], sem.at[0, n, c]) for n, c, at in cuts]
    writes = [pltpu.make_async_copy(bufs[n].at[at], outs[n].at[at], sem.at[1, n, c]) for n, c, at in cuts]
    for copy in reads:
        copy.start()
    for read, write in zip(reads, writes):
        read.wait()
        write.start()
    for copy in writes:
        copy.wait()


def per_device(queries, keys, values, out_grad, tissue):
    width = queries.shape[-1]
    groups = width // LANES
    flat = (OWN, width)
    any_spec = pl.BlockSpec(memory_space=pl.ANY)
    dma = pltpu.SemaphoreType.DMA
    outs = pl.pallas_call(
        functools.partial(kernel, groups, lax.axis_size("gx"), lax.axis_size("gy")),
        out_shape=[jax.ShapeDtypeStruct(flat, BF)] * 4,
        in_specs=[any_spec] * 4 + [pl.BlockSpec(memory_space=pltpu.VMEM)],
        out_specs=[any_spec] * 4,
        scratch_shapes=[
            pltpu.VMEM((groups, ROWS, 2 * LANES), BF),
            pltpu.VMEM((groups, OWN, LANES), BF),
            pltpu.VMEM((groups, OWN, LANES), BF),
            pltpu.VMEM((KEYS, LANES), BF),
            pltpu.VMEM((OWN, LANES), BF),
            pltpu.VMEM((2 * SLOTS, CENTER), BF),
            pltpu.VMEM((CENTER, 2 * SLOTS), BF),
            pltpu.VMEM((3, LANES, LANES), BF),
            pltpu.VMEM((16, LANES), F32),
            pltpu.VMEM((8, OWN), F32),
            pltpu.VMEM((groups, 2 * SLOTS, 2 * LANES), BF),
            pltpu.VMEM((3, CENTER, 2 * LANES), F32),
            pltpu.VMEM((groups, OWN, 2 * LANES), F32),
            pltpu.VMEM((groups, STRIP, 2 * LANES), F32),
            pltpu.VMEM((groups, 2 * SLOTS, 2 * LANES), BF),
            pltpu.VMEM((groups, 2 * SLOTS, 2 * LANES), BF),
            pltpu.VMEM((groups, STRIP, 2 * LANES), BF),
            pltpu.VMEM((groups, STRIP, 2 * LANES), BF),
            pltpu.VMEM((groups, OWN, 2 * LANES), BF),
            pltpu.VMEM((groups, OWN, 2 * LANES), BF),
            pltpu.VMEM((groups, OWN, LANES), BF),
            pltpu.VMEM((groups, OWN, LANES), BF),
            pltpu.VMEM((groups, OWN, LANES), BF),
            pltpu.VMEM((groups, OWN, LANES), BF),
            pltpu.VMEM((groups, SLOTS, 2 * LANES), BF),
            dma((groups, 4)), dma((groups, 4)),
            dma((groups, 2)), dma((groups, 2)), dma((groups,)), dma((groups,)),
            dma((groups, 2)), dma((groups, 2)), dma((groups, 2)), dma((groups, 2)),
            dma((groups,)), dma((groups,)), dma((groups,)), dma((groups,)),
            dma((2,)), dma((2,)), dma((2,)), dma((2,)),
            dma((groups,)), dma((groups,)),
        ],
        compiler_params=pltpu.CompilerParams(
            collective_id=0, has_side_effects=True, vmem_limit_bytes=56 * 1024 * 1024
        ),
    )(
        keys.reshape(flat), values.reshape(flat), queries.reshape(flat), out_grad.reshape(flat),
        tissue,
    )
    outs = pl.pallas_call(
        write_out,
        out_shape=[jax.ShapeDtypeStruct(flat, BF)] * 4,
        in_specs=[any_spec] * 4,
        out_specs=[any_spec] * 4,
        scratch_shapes=[pltpu.VMEM(flat, BF)] * 4 + [dma((2, 4, 4))],
    )(*outs)
    return tuple(out.reshape(queries.shape) for out in outs)


def solution(mesh):
    tokens = P("gy", "gx", None)
    return jax.shard_map(
        per_device, mesh=mesh, in_specs=(tokens,) * 4 + (P("gy", "gx"),),
        out_specs=(tokens,) * 4, check_vma=False,
    )
```
